32 devices in a mesh: dp: 2 (over core), fsdp: 4 (over y, x), ctx: 4 (over z).
Axes of the slice: x: 2, y: 2, z: 4, core: 2. Of those that a mesh axis runs over, the one named last changes fastest.
Arguments:
- tokens: bfloat16 [8, 1024, 960], P(('dp', 'fsdp'), 'ctx'), may hold values from -6 to 6
- positions: int32 [8, 1024], P(('dp', 'fsdp'), 'ctx'), may hold values from 0 to 2046, as said below
- gain_attn: float32 [960], replicated, may hold values from 0.25 to 1.75
- gain_mlp: float32 [960], replicated, may hold values from 0.25 to 1.75
- w_qkv: bfloat16 [960, 1600], P('fsdp'), may hold values from -0.1875 to 0.1875
- w_out: bfloat16 [960, 960], P('fsdp'), may hold values from -0.75 to 0.75
- w_gu: bfloat16 [960, 5120], P('fsdp'), may hold values from -0.1875 to 0.1875
- w_down: bfloat16 [2560, 960], P('fsdp'), may hold values from -0.125 to 0.125
- cotangent: bfloat16 [8, 1024, 960], P(('dp', 'fsdp'), 'ctx'), may hold values from -6 to 6
Outputs:
- out_tokens: float32 [8, 1024, 960], P(('dp', 'fsdp'), 'ctx')
- grad_tokens: float32 [8, 1024, 960], P(('dp', 'fsdp'), 'ctx')
- grad_gain_attn: float32 [960], P(('fsdp', 'ctx'))
- grad_gain_mlp: float32 [960], P(('fsdp', 'ctx'))
- grad_qkv: float32 [960, 1600], P(('fsdp', 'ctx'), 'dp')
- grad_out: float32 [960, 960], P(('fsdp', 'ctx'), 'dp')
- grad_gu: float32 [960, 5120], P(('fsdp', 'ctx'), 'dp')
- grad_down: float32 [2560, 960], P(('fsdp', 'ctx'), 'dp')
The draws below stay inside these ranges and needn't reach their ends.
Inputs may be any that keep to these rules, and one draw needn't show every extreme that they name: `positions`: strictly increasing along each sequence; each sequence starts at 0 and ends at 2046.
All inputs are finite; a program needn't handle non-finite values.
Results may differ from the reference program's by a relative error of at most 0.02.
Values may be sent and summed in bfloat16 or wider, within the bound.
A program may use at most 128 MiB of HBM per device.

```python
import jax
import jax.numpy as jnp
from jax import lax

D = 960
HEADS = 15
KV_HEADS = 5
HD = 64
FF = 2560
SEQ = 1024
SEQS = 8


def one_sequence(key):
    chosen = jax.random.permutation(key, 2 * SEQ - 3)[:SEQ - 2] + 1
    middle = jnp.sort(chosen).astype(jnp.int32)
    first = jnp.zeros((1,), jnp.int32)
    last = jnp.full((1,), 2 * SEQ - 2, jnp.int32)
    return jnp.concatenate([first, middle, last])


def draw_positions(key, part):
    key = jax.random.fold_in(key, 7)
    seq_keys = jax.random.split(key, SEQS)
    return jax.vmap(one_sequence)(seq_keys).astype(jnp.int32)


def steps_of(key, shape, pieces, low, top_value):
    level, own = 1.0, jax.random.fold_in(key, 6)
    for dim, parts in pieces:
        draws = jnp.exp(jax.random.uniform(jax.random.fold_in(own, dim), (parts,), jnp.float32, low / len(pieces), top_value / len(pieces)))
        level = level * jnp.repeat(draws, shape[dim] // parts).reshape([-1 if axis == dim else 1 for axis in range(len(shape))])
    return level


def noise(rng, shape, scale, most, cuts=(), kind=jnp.bfloat16):
    result = scale * jax.random.normal(rng, shape, jnp.float32)
    if cuts:
        result = result * steps_of(rng, shape, cuts, -0.22, 0.18)
    return jnp.clip(result, -most, most).astype(kind)


def setup_inputs(seed: int = 0) -> dict:
    keys = jax.random.split(jax.random.key(seed), 10)
    return {
        "tokens": noise(keys[0], (SEQS, SEQ, D), 1.0, 6.0, ((0, 8), (1, 4))),
        "positions": draw_positions(jax.random.fold_in(keys[9], 71), 0),
        "gain_attn": jnp.clip(1.0 + 0.15 * jax.random.normal(keys[2], (D,), jnp.float32), 0.25, 1.75),
        "gain_mlp": jnp.clip(1.0 + 0.15 * jax.random.normal(keys[3], (D,), jnp.float32), 0.25, 1.75),
        "w_qkv": noise(keys[4], (D, D + 2 * KV_HEADS * HD), D ** -0.5, 0.1875, ((0, 4),)),
        "w_out": noise(keys[5], (D, D), HD ** -0.5, 0.75, ((0, 4),)),
        "w_gu": noise(keys[6], (D, 2 * FF), D ** -0.5, 0.1875, ((0, 4),)),
        "w_down": noise(keys[7], (FF, D), FF ** -0.5, 0.125, ((0, 4),)),
        "cotangent": noise(keys[8], (SEQS, SEQ, D), 1.0, 6.0, ((0, 8), (1, 4))),
    }


EPSILON = 1e-05
HIGHEST = lax.Precision.HIGHEST

@jax.custom_vjp
def low(v):
    return lax.optimization_barrier(v.astype(jnp.bfloat16)).astype(jnp.float32)

@jax.custom_vjp
def low_back(v):
    return v

def low_keep(v):
    return (low(v), None)

def low_pass(kept, grad):
    return (grad,)

def back_keep(v):
    return (v, None)

def back_low(kept, grad):
    return (low(grad),)
low.defvjp(low_keep, low_pass)
low_back.defvjp(back_keep, back_low)

def rotate(values, places, direction):
    half_dim = values.shape[-1] // 2
    frequency = 10000.0 ** (-jnp.arange(half_dim, dtype=jnp.float32) / half_dim)
    angles = places.astype(jnp.float32)[:, None] * frequency[None, :]
    cosine = jnp.cos(angles)[:, None, :]
    sine_part = direction * jnp.sin(angles)[:, None, :]
    front_half = values[..., :half_dim]
    back_half = values[..., half_dim:]
    return jnp.concatenate([front_half * cosine - back_half * sine_part, back_half * cosine + front_half * sine_part], axis=-1)

def normalize(values, gain):
    return values * lax.rsqrt(lax.optimization_barrier(jnp.mean(values * values, axis=-1, keepdims=True)) + EPSILON) * gain

def block_layer(inputs, places, gain_attn, gain_mlp, w_qkv, w_out, w_gu, w_down):
    length = inputs.shape[0]
    kv_width = KV_HEADS * HD
    group_size = HEADS // KV_HEADS
    normed = low(normalize(inputs, gain_attn))
    project = low_back(jnp.dot(normed, w_qkv, precision=HIGHEST))
    queries = low(rotate(project[:, :D].reshape(length, HEADS, HD), places, 1.0))
    key_block = low(rotate(project[:, D:D + kv_width].reshape(length, KV_HEADS, HD), places, 1.0))
    values = low(project[:, D + kv_width:].reshape(length, KV_HEADS, HD))
    grouped = queries.reshape(length, KV_HEADS, group_size, HD)
    scores = low_back(HD ** (-0.5) * jnp.einsum('qkgd,skd->kgqs', grouped, key_block, precision=HIGHEST))
    allowed = jnp.arange(length)[None, :] <= jnp.arange(length)[:, None]
    scores = jnp.where(allowed, scores, -1e+30)
    row_max = lax.optimization_barrier(jnp.max(scores, axis=-1, keepdims=True))
    exponent = jnp.exp(scores - row_max)
    probability = exponent / lax.optimization_barrier(jnp.sum(exponent, axis=-1, keepdims=True))
    attended = jnp.einsum('kgqs,skd->qkgd', low(probability), values, precision=HIGHEST).reshape(length, D)
    attended = low(low_back(attended))
    hidden_state = inputs + low_back(jnp.dot(attended, w_out, precision=HIGHEST))
    normed_two = low(normalize(hidden_state, gain_mlp))
    gate_up = low_back(jnp.dot(normed_two, w_gu, precision=HIGHEST))
    activated = low(jax.nn.silu(gate_up[:, :FF]) * gate_up[:, FF:])
    return hidden_state + low_back(jnp.dot(activated, w_down, precision=HIGHEST))

def reference(tokens, positions, gain_attn, gain_mlp, w_qkv, w_out, w_gu, w_down, cotangent):
    inputs = tokens.astype(jnp.float32)
    parameters = (gain_attn.astype(jnp.float32), gain_mlp.astype(jnp.float32), w_qkv.astype(jnp.float32), w_out.astype(jnp.float32), w_gu.astype(jnp.float32), w_down.astype(jnp.float32))
    layer_step = jax.checkpoint(block_layer)

    def forward(inputs, parameters):

        def advance(unused, sequence_item):
            return (unused, layer_step(sequence_item[0], sequence_item[1], *parameters))
        return lax.scan(advance, None, (inputs, positions))[1]
    outputs, pullback = jax.vjp(forward, inputs, parameters)
    grad_inputs, grads = pullback(cotangent.astype(jnp.float32))
    return (outputs, grad_inputs, grads[0], grads[1], grads[2], grads[3], grads[4], grads[5])
```

```python
import jax
import jax.numpy as jnp
from jax import lax
from jax.experimental import pallas as pl
from jax.experimental.pallas import tpu as pltpu
from jax.sharding import PartitionSpec as P

D = 960
HEADS = 15
KV_HEADS = 5
HD = 64
FF = 2560
GROUP = HEADS // KV_HEADS
KVW = KV_HEADS * HD
EPSILON = 1e-05
F32 = jnp.float32
BF16 = jnp.bfloat16


def dot(a, b, ca, cb):
    return lax.dot_general(a, b, (((ca,), (cb,)), ((), ())), preferred_element_type=F32)


def normalize(values, gain):
    return values * lax.rsqrt(jnp.mean(values * values, axis=-1, keepdims=True) + EPSILON) * gain


def angles_of(places):
    half = HD // 2
    frequency = 10000.0 ** (-jnp.arange(half, dtype=F32) / half)
    angles = frequency[:, None] * places.astype(F32)[None, :]
    return jnp.cos(angles), jnp.sin(angles)


def rotate(values, cosine, sine):
    length = values.shape[1]
    parts = values.reshape(-1, 2, HD // 2, length)
    front, back = parts[:, 0], parts[:, 1]
    turned = jnp.stack([front * cosine - back * sine, back * cosine + front * sine], axis=1)
    return turned.reshape(-1, length)


def keys_first(kv, which):
    pieces = [kv[c, which] for c in range(kv.shape[0])]
    return (
        jnp.concatenate([piece.T for piece in pieces], axis=0),
        jnp.concatenate(pieces, axis=1),
    )


def allowed_of(keys, rows):
    start = lax.axis_index("ctx") * rows
    key_at = lax.broadcasted_iota(jnp.int32, (keys, rows), 0)
    row_at = lax.broadcasted_iota(jnp.int32, (keys, rows), 1)
    return key_at <= row_at + start


def forward_kernel(q_ref, kv_ref, att_ref, lse_ref):
    rows = q_ref.shape[1]
    kv = kv_ref[...]
    keys, _ = keys_first(kv, 0)
    values_t = jnp.concatenate([kv[c, 1] for c in range(kv.shape[0])], axis=1)
    allowed = allowed_of(keys.shape[0], rows)
    for h in range(GROUP):
        q = q_ref[h * HD : (h + 1) * HD, :]
        scores = jnp.where(allowed, dot(keys, q, 1, 0), -1e30)
        row_max = jnp.max(scores, axis=0, keepdims=True)
        exponent = jnp.exp(scores - row_max)
        total = jnp.sum(exponent, axis=0, keepdims=True)
        att = dot(values_t, exponent.astype(BF16), 1, 0) / total
        att_ref[h * HD : (h + 1) * HD, :] = att.astype(BF16)
        lse_ref[0, h : h + 1, :] = row_max + jnp.log(total)


def backward_kernel(q_ref, kv_ref, g_ref, lse_ref, dq_ref, dkv_ref):
    rows = q_ref.shape[1]
    kv = kv_ref[...]
    parts = kv.shape[0]
    keys, keys_t = keys_first(kv, 0)
    values, _ = keys_first(kv, 1)
    allowed = allowed_of(keys.shape[0], rows)
    dk = jnp.zeros((HD, keys.shape[0]), F32)
    dv = jnp.zeros((HD, keys.shape[0]), F32)
    for h in range(GROUP):
        q = q_ref[h * HD : (h + 1) * HD, :]
        g = g_ref[h * HD : (h + 1) * HD, :]
        scores = jnp.where(allowed, dot(keys, q, 1, 0), -1e30)
        prob = jnp.exp(scores - lse_ref[0, h : h + 1, :])
        dprob = dot(values, g, 1, 0)
        inner = jnp.sum(dprob * prob, axis=0, keepdims=True)
        ds = (prob * (dprob - inner)).astype(BF16)
        dq_ref[h * HD : (h + 1) * HD, :] = dot(keys_t, ds, 1, 0) * (HD**-0.5)
        dk = dk + dot(q, ds, 1, 1)
        dv = dv + dot(g, prob.astype(BF16), 1, 1)
    for c in range(parts):
        dkv_ref[c, 0] = dk[:, c * rows : (c + 1) * rows].astype(BF16)
        dkv_ref[c, 1] = dv[:, c * rows : (c + 1) * rows].astype(BF16)


def attention_specs(parts, rows):
    q_spec = pl.BlockSpec((GROUP * HD, rows), lambda g: (g, 0))
    kv_spec = pl.BlockSpec((parts, 2, HD, rows), lambda g: (0, 0, g, 0))
    lse_spec = pl.BlockSpec((1, GROUP, rows), lambda g: (g, 0, 0))
    return q_spec, kv_spec, lse_spec


def attention_forward(q, kv):
    parts, rows = kv.shape[0], q.shape[1]
    q_spec, kv_spec, lse_spec = attention_specs(parts, rows)
    work = parts * rows * rows * HD * HEADS
    return pl.pallas_call(
        forward_kernel,
        grid=(KV_HEADS,),
        in_specs=[q_spec, kv_spec],
        out_specs=[q_spec, lse_spec],
        out_shape=[
            jax.ShapeDtypeStruct((D, rows), BF16),
            jax.ShapeDtypeStruct((KV_HEADS, GROUP, rows), F32),
        ],
        compiler_params=pltpu.CompilerParams(vmem_limit_bytes=40 * 2**20),
        cost_estimate=pl.CostEstimate(
            flops=16 * work, bytes_accessed=3 * 2**20, transcendentals=work // HD
        ),
    )(q, kv)


def attention_backward(q, kv, g, lse):
    parts, rows = kv.shape[0], q.shape[1]
    q_spec, kv_spec, lse_spec = attention_specs(parts, rows)
    work = parts * rows * rows * HD * HEADS
    return pl.pallas_call(
        backward_kernel,
        grid=(KV_HEADS,),
        in_specs=[q_spec, kv_spec, q_spec, lse_spec],
        out_specs=[q_spec, kv_spec],
        out_shape=[
            jax.ShapeDtypeStruct((D, rows), F32),
            jax.ShapeDtypeStruct(kv.shape, BF16),
        ],
        compiler_params=pltpu.CompilerParams(vmem_limit_bytes=40 * 2**20),
        cost_estimate=pl.CostEstimate(
            flops=40 * work, bytes_accessed=5 * 2**20, transcendentals=work // HD
        ),
    )(q, kv, g, lse)


def halves(grad, dp):
    rows, columns = grad.shape
    return grad.reshape(rows, dp, columns // dp).transpose(1, 0, 2)


def over_dp(grad):
    return lax.psum_scatter(grad, "dp", scatter_dimension=0, tiled=True)


def shards(tokens, positions, gain_attn, gain_mlp, w_qkv, w_out, w_gu, w_down, cotangent):
    rows = tokens.shape[1]
    fsdp, ctx, dp = lax.axis_size("fsdp"), lax.axis_size("ctx"), lax.axis_size("dp")
    part = FF // fsdp
    own = D // fsdp
    slim = D // (fsdp * ctx)
    inputs = tokens[0].astype(F32)
    cosine, sine = angles_of(positions[0])
    full_qkv = lax.all_gather(w_qkv, "fsdp", axis=0, tiled=True)
    full_out = lax.all_gather(w_out, "fsdp", axis=0, tiled=True)
    cot_all = lax.all_gather(cotangent[0], "fsdp", axis=0, tiled=True)
    gu_cut = w_gu.reshape(own, 2, fsdp, part).transpose(2, 0, 1, 3).reshape(fsdp, own, 2 * part)
    gu_part = lax.all_to_all(gu_cut, "fsdp", 0, 0).reshape(D, 2 * part)

    normed = normalize(inputs, gain_attn).astype(BF16)
    project = dot(full_qkv, normed, 0, 1)
    turned = rotate(project[: D + KVW], cosine, sine)
    queries = (turned[:D] * (HD**-0.5)).astype(BF16)
    local_kv = jnp.concatenate([turned[D:].astype(BF16), project[D + KVW :].astype(BF16)], axis=0)
    every_kv = lax.all_gather(local_kv, "ctx", axis=0, tiled=False).reshape(ctx, 2, KVW, rows)
    attended, lse = attention_forward(queries, every_kv)
    hidden = inputs + dot(attended, full_out, 0, 0)
    normed_two = normalize(hidden, gain_mlp).astype(BF16)

    two_all = lax.all_gather(normed_two, "fsdp", axis=0, tiled=True)
    gate_up = dot(two_all, gu_part, 1, 0)
    gate, up = gate_up[:, :part], gate_up[:, part:]
    activated, swish_back = jax.vjp(lambda a, b: jax.nn.silu(a) * b, gate, up)
    activated = activated.astype(BF16)
    grad_activated = dot(cot_all, w_down, 1, 1)
    grad_gate, grad_up = swish_back(grad_activated)
    grad_gate_up = jnp.concatenate([grad_gate, grad_up], axis=1).astype(BF16)
    two_part = dot(grad_gate_up, gu_part, 1, 1).astype(BF16)
    grad_two = lax.psum_scatter(two_part, "fsdp", scatter_dimension=0, tiled=True).astype(F32)
    down_part = dot(activated, w_down, 1, 0).astype(BF16)
    down_sum = lax.psum_scatter(down_part, "fsdp", scatter_dimension=0, tiled=True)
    outputs = hidden + down_sum.astype(F32)
    grad_down = dot(activated, cot_all, 0, 0).astype(BF16)
    grad_gu = dot(two_all, grad_gate_up, 0, 0).astype(BF16)

    result_down = lax.psum_scatter(
        over_dp(halves(grad_down, dp)).reshape(ctx, part // ctx, D // dp),
        "ctx",
        scatter_dimension=0,
        tiled=True,
    )[0]
    if dp == 2:
        gu_cols = over_dp(halves(grad_gu, dp))[0]
    else:
        gu_cols = grad_gu
    gu_rows = lax.psum_scatter(
        gu_cols.reshape(fsdp, ctx, slim, -1).transpose(1, 0, 2, 3),
        "ctx",
        scatter_dimension=0,
        tiled=True,
    )[0]
    gu_rows = lax.all_to_all(gu_rows, "fsdp", 0, 0)
    if dp == 2:
        result_gu = gu_rows.transpose(1, 0, 2).reshape(slim, FF)
    else:
        gu_rows = gu_rows.reshape(fsdp, slim, 2, part).transpose(1, 2, 0, 3).reshape(slim, 2 * FF)
        result_gu = lax.psum_scatter(gu_rows, "dp", scatter_dimension=1, tiled=True)

    grad_rows = cotangent[0].astype(F32)
    _, norm_back_two = jax.vjp(normalize, hidden, gain_mlp)
    grad_hidden_part, grad_gain_mlp = norm_back_two(grad_two)
    grad_hidden = grad_rows + grad_hidden_part
    grad_attn = grad_hidden.astype(BF16)
    grad_attended = dot(full_out, grad_attn, 1, 1).astype(BF16)
    grad_out = dot(attended, grad_attn, 1, 0).astype(BF16)
    grad_queries, kv_grads = attention_backward(queries, every_kv, grad_attended, lse)
    own_kv = lax.psum_scatter(
        kv_grads.reshape(ctx, 2 * KVW, rows), "ctx", scatter_dimension=0, tiled=True
    )[0].astype(F32)
    grad_project = jnp.concatenate(
        [
            rotate(grad_queries, cosine, -sine),
            rotate(own_kv[:KVW], cosine, -sine),
            own_kv[KVW:],
        ],
        axis=0,
    ).astype(BF16)
    grad_normed = dot(grad_project, full_qkv, 0, 1)
    grad_qkv = dot(normed, grad_project, 0, 1).astype(BF16)
    _, norm_back_one = jax.vjp(normalize, inputs, gain_attn)
    grad_input_part, grad_gain_attn = norm_back_one(grad_normed)
    grad_inputs = grad_hidden + grad_input_part

    both = over_dp(jnp.concatenate([halves(grad_qkv, dp), halves(grad_out, dp)], axis=2))
    both = lax.psum_scatter(
        both.reshape(fsdp * ctx, slim, -1), ("fsdp", "ctx"), scatter_dimension=0, tiled=True
    )[0]
    wide = w_qkv.shape[1] // dp
    gains = lax.psum(jnp.stack([grad_gain_attn, grad_gain_mlp]), ("dp", "fsdp", "ctx"))
    place = lax.axis_index("fsdp") * ctx + lax.axis_index("ctx")
    gains = lax.dynamic_slice(gains, (0, place * slim), (2, slim))
    return (
        outputs[None],
        grad_inputs[None],
        gains[0],
        gains[1],
        both[:, :wide].astype(F32),
        both[:, wide:].astype(F32),
        result_gu.astype(F32),
        result_down.astype(F32),
    )


def solution(mesh):
    placed = (
        P(("dp", "fsdp"), "ctx", None),
        P(("dp", "fsdp"), "ctx"),
        P(),
        P(),
        P("fsdp", None),
        P("fsdp", None),
        P("fsdp", None),
        P("fsdp", None),
        P(("dp", "fsdp"), "ctx", None),
    )
    return jax.shard_map(
        shards,
        mesh=mesh,
        in_specs=placed,
        out_specs=(
            P(("dp", "fsdp"), "ctx", None),
            P(("dp", "fsdp"), "ctx", None),
            P(("fsdp", "ctx")),
            P(("fsdp", "ctx")),
            P(("fsdp", "ctx"), "dp"),
            P(("fsdp", "ctx"), "dp"),
            P(("fsdp", "ctx"), "dp"),
            P(("fsdp", "ctx"), "dp"),
        ),
        check_vma=False,
    )
```

```python
import functools

import jax
import jax.numpy as jnp
from jax import lax
from jax.experimental import pallas as pl
from jax.experimental.pallas import tpu as pltpu
from jax.sharding import PartitionSpec as P

D = 960
HEADS = 15
KV_HEADS = 5
HD = 64
FF = 2560
GROUP = HEADS // KV_HEADS
KVW = KV_HEADS * HD
EPSILON = 1e-05
F32 = jnp.float32
BF16 = jnp.bfloat16


def dot(a, b, ca, cb):
    return lax.dot_general(a, b, (((ca,), (cb,)), ((), ())), preferred_element_type=F32)


def normalize(values, gain):
    return values * lax.rsqrt(jnp.mean(values * values, axis=-1, keepdims=True) + EPSILON) * gain


def angles_of(places):
    half = HD // 2
    frequency = 10000.0 ** (-jnp.arange(half, dtype=F32) / half)
    angles = frequency[:, None] * places.astype(F32)[None, :]
    return jnp.cos(angles), jnp.sin(angles)


def rotate(values, cosine, sine):
    length = values.shape[1]
    parts = values.reshape(-1, 2, HD // 2, length)
    front, back = parts[:, 0], parts[:, 1]
    turned = jnp.stack([front * cosine - back * sine, back * cosine + front * sine], axis=1)
    return turned.reshape(-1, length)


def keys_first(kv, which):
    pieces = [kv[c, which] for c in range(kv.shape[0])]
    return (
        jnp.concatenate([piece.T for piece in pieces], axis=0),
        jnp.concatenate(pieces, axis=1),
    )


def allowed_of(keys, rows):
    start = lax.axis_index("ctx") * rows
    key_at = lax.broadcasted_iota(jnp.int32, (keys, rows), 0)
    row_at = lax.broadcasted_iota(jnp.int32, (keys, rows), 1)
    return key_at <= row_at + start


def backward_kernel(q_ref, kv_ref, g_ref, lse_ref, dq_ref, dkv_ref):
    rows = q_ref.shape[1]
    kv = kv_ref[...]
    parts = kv.shape[0]
    keys, keys_t = keys_first(kv, 0)
    values, _ = keys_first(kv, 1)
    allowed = allowed_of(keys.shape[0], rows)
    dk = jnp.zeros((HD, keys.shape[0]), F32)
    dv = jnp.zeros((HD, keys.shape[0]), F32)
    for h in range(GROUP):
        q = q_ref[h * HD : (h + 1) * HD, :]
        g = g_ref[h * HD : (h + 1) * HD, :]
        scores = jnp.where(allowed, dot(keys, q, 1, 0), -1e30)
        prob = jnp.exp(scores - lse_ref[0, h : h + 1, :])
        dprob = dot(values, g, 1, 0)
        inner = jnp.sum(dprob * prob, axis=0, keepdims=True)
        ds = (prob * (dprob - inner)).astype(BF16)
        dq_ref[h * HD : (h + 1) * HD, :] = dot(keys_t, ds, 1, 0) * (HD**-0.5)
        dk = dk + dot(q, ds, 1, 1)
        dv = dv + dot(g, prob.astype(BF16), 1, 1)
    for c in range(parts):
        dkv_ref[c, 0] = dk[:, c * rows : (c + 1) * rows].astype(BF16)
        dkv_ref[c, 1] = dv[:, c * rows : (c + 1) * rows].astype(BF16)


def attention_specs(parts, rows):
    q_spec = pl.BlockSpec((GROUP * HD, rows), lambda g: (g, 0))
    kv_spec = pl.BlockSpec((parts, 2, HD, rows), lambda g: (0, 0, g, 0))
    lse_spec = pl.BlockSpec((1, GROUP, rows), lambda g: (g, 0, 0))
    return q_spec, kv_spec, lse_spec


def attention_backward(q, kv, g, lse):
    parts, rows = kv.shape[0], q.shape[1]
    q_spec, kv_spec, lse_spec = attention_specs(parts, rows)
    work = parts * rows * rows * HD * HEADS
    return pl.pallas_call(
        backward_kernel,
        grid=(KV_HEADS,),
        in_specs=[q_spec, kv_spec, q_spec, lse_spec],
        out_specs=[q_spec, kv_spec],
        out_shape=[
            jax.ShapeDtypeStruct((D, rows), F32),
            jax.ShapeDtypeStruct(kv.shape, BF16),
        ],
        compiler_params=pltpu.CompilerParams(vmem_limit_bytes=40 * 2**20),
        cost_estimate=pl.CostEstimate(
            flops=40 * work, bytes_accessed=5 * 2**20, transcendentals=work // HD
        ),
    )(q, kv, g, lse)


def halves(grad, dp):
    rows, columns = grad.shape
    return grad.reshape(rows, dp, columns // dp).transpose(1, 0, 2)


MESH = pl.DeviceIdType.MESH


def peer_of(axis, k):
    size = lax.axis_size(axis)
    return lax.rem(lax.axis_index(axis) + k, size)


def greet(axes):
    barrier = pltpu.get_barrier_semaphore()
    count = 0
    for axis in axes:
        for k in range(1, lax.axis_size(axis)):
            pl.semaphore_signal(
                barrier, inc=1, device_id={axis: peer_of(axis, k)}, device_id_type=MESH
            )
            count += 1
    pl.semaphore_wait(barrier, count)


def send(src, dst, sems, at, axis, k):
    copy = pltpu.make_async_remote_copy(
        src_ref=src,
        dst_ref=dst,
        send_sem=sems[0].at[at],
        recv_sem=sems[1].at[at],
        device_id={axis: peer_of(axis, k)},
        device_id_type=MESH,
    )
    copy.start()
    return copy


def swap_kernel(plan, *refs):
    count = len(plan)
    ins, outs = refs[:count], refs[count : 2 * count]
    local_sem, send_sem, recv_sem = refs[2 * count :]
    greet(sorted({axis for axis, _ in plan}))
    copies, at = [], 0
    for i, (axis, gather) in enumerate(plan):
        me = lax.axis_index(axis)
        own = ins[i] if gather else ins[i].at[me]
        copy = pltpu.make_async_copy(own, outs[i].at[me], local_sem.at[i])
        copy.start()
        copies.append(copy)
        for k in range(1, lax.axis_size(axis)):
            src = ins[i] if gather else ins[i].at[peer_of(axis, k)]
            copies.append(send(src, outs[i].at[me], (send_sem, recv_sem), at, axis, k))
            at += 1
    for copy in copies:
        copy.wait()


def swap(collective_id, *items):
    plan = [(axis, gather) for _, axis, gather in items]
    shapes = [
        jax.ShapeDtypeStruct(((lax.axis_size(axis),) + x.shape) if gather else x.shape, x.dtype)
        for x, axis, gather in items
    ]
    total = sum(lax.axis_size(axis) - 1 for axis, _ in plan)
    size = sum(shape.size * shape.dtype.itemsize for shape in shapes)
    return pl.pallas_call(
        functools.partial(swap_kernel, plan),
        in_specs=[pl.BlockSpec(memory_space=pl.ANY)] * len(plan),
        out_specs=[pl.BlockSpec(memory_space=pl.ANY)] * len(plan),
        out_shape=shapes,
        scratch_shapes=[
            pltpu.SemaphoreType.DMA((len(plan),)),
            pltpu.SemaphoreType.DMA((total,)),
            pltpu.SemaphoreType.DMA((total,)),
        ],
        compiler_params=pltpu.CompilerParams(collective_id=collective_id, has_side_effects=True),
        cost_estimate=pl.CostEstimate(flops=0, bytes_accessed=20 * size, transcendentals=0),
    )(*[x for x, _, _ in items])


def front_kernel(
    shared, qkv_in, out_in, gu_in, cot_in, normed, cosine, sine,
    qkv, out_all, gu_all, cot_all, q_ref, kv, att_ref, lse_ref,
    project, local_sem, send_sem, recv_sem, pass_send, pass_recv,
):
    fsdp, ctx = lax.axis_size("fsdp"), lax.axis_size("ctx")
    me, here = lax.axis_index("fsdp"), lax.axis_index("ctx")
    side = lax.axis_index("dp")
    rows = normed.shape[1]
    sems, pass_sems = (send_sem, recv_sem), (pass_send, pass_recv)
    greet(("fsdp", "ctx") + (("dp",) if shared else ()))
    locals_ = [
        pltpu.make_async_copy(qkv_in, qkv.at[me], local_sem.at[0]),
        pltpu.make_async_copy(out_in, out_all.at[me], local_sem.at[1]),
        pltpu.make_async_copy(gu_in.at[me], gu_all.at[me], local_sem.at[2]),
        pltpu.make_async_copy(cot_in, cot_all.at[me], local_sem.at[3]),
    ]
    for copy in locals_:
        copy.start()
    halves_of = lambda ref: ref.at[side] if shared else ref
    peers = range(1, fsdp)
    first = [
        send(halves_of(qkv_in), halves_of(qkv.at[me]), sems, k - 1, "fsdp", k) for k in peers
    ]
    rest, passed = [], []

    def hand_over(ref, base, arrivals):
        for k, copy in zip(peers, arrivals):
            copy.wait_recv()
            if shared:
                block = ref.at[lax.rem(me - k + fsdp, fsdp), side]
                passed.append(send(block, block, pass_sems, base + k - 1, "dp", 1))

    hand_over(qkv, 0, first)
    base = fsdp - 1
    seconds = [
        send(halves_of(out_in), halves_of(out_all.at[me]), sems, base + k - 1, "fsdp", k)
        for k in peers
    ]
    thirds = [
        send(
            halves_of(gu_in.at[peer_of("fsdp", k)]), halves_of(gu_all.at[me]), sems,
            2 * base + k - 1, "fsdp", k,
        )
        for k in peers
    ]
    lasts = [send(cot_in, cot_all.at[me], sems, 3 * base + k - 1, "fsdp", k) for k in peers]
    for copy in passed:
        copy.wait_recv()
    locals_[0].wait()
    blocks = 2 * fsdp
    total = jnp.zeros(project.shape[::-1], F32)
    for b in range(blocks):
        total = total + dot(normed[b], qkv[b // 2, b % 2], 1, 0)
    project[...] = total.T
    half = HD // 2
    cos, sin = cosine[...], sine[...]
    mine = kv.at[here]

    def turn(h, carry):
        start = pl.multiple_of(h * HD, HD)
        a = project[pl.ds(start, half), :]
        b = project[pl.ds(start + half, half), :]
        q_ref[pl.ds(start, HD), :] = (
            jnp.concatenate([a * cos - b * sin, b * cos + a * sin], axis=0) * (HD**-0.5)
        ).astype(BF16)
        return carry

    for h in range(KV_HEADS):
        at = D + h * HD
        a, b = project[at : at + half, :], project[at + half : at + HD, :]
        mine[0, h * HD : (h + 1) * HD, :] = jnp.concatenate(
            [a * cos - b * sin, b * cos + a * sin], axis=0
        ).astype(BF16)
    mine[1, :, :] = project[D + KVW :, :].astype(BF16)
    kvs = [
        send(mine, mine, sems, 4 * base + k - 1, "ctx", k) for k in range(1, ctx)
    ]
    lax.fori_loop(0, HEADS, turn, 0)
    hand_over(out_all, base, seconds)
    for copy in kvs:
        copy.wait()
    allowed = allowed_of(ctx * rows, rows)

    def attend(g, carry):
        at = pl.ds(pl.multiple_of(g * HD, HD), HD)
        keys = jnp.concatenate([kv[c, 0, at, :].T for c in range(ctx)], axis=0)
        values_t = jnp.concatenate([kv[c, 1, at, :] for c in range(ctx)], axis=1)
        for h in range(GROUP):
            spot = pl.ds(pl.multiple_of((g * GROUP + h) * HD, HD), HD)
            scores = jnp.where(allowed, dot(keys, q_ref[spot, :], 1, 0), -1e30)
            row_max = jnp.max(scores, axis=0, keepdims=True)
            exponent = jnp.exp(scores - row_max)
            sums = jnp.sum(exponent, axis=0, keepdims=True)
            att = dot(values_t, exponent.astype(BF16), 1, 0) / sums
            att_ref[spot, :] = att.astype(BF16)
            lse_ref[g, h : h + 1, :] = row_max + jnp.log(sums)
        return carry

    lax.fori_loop(0, KV_HEADS, attend, 0)
    hand_over(gu_all, 2 * base, thirds)
    for copy in lasts:
        copy.wait_recv()
    for copy in first + seconds + thirds + lasts:
        copy.wait_send()
    for i, copy in enumerate(passed):
        copy.wait_send()
        if i >= base:
            copy.wait_recv()
    for copy in locals_[1:]:
        copy.wait()


def front(qkv_in, out_in, gu_in, cot_in, normed, cosine, sine):
    fsdp, ctx, dp = lax.axis_size("fsdp"), lax.axis_size("ctx"), lax.axis_size("dp")
    rows = normed.shape[1]
    columns = qkv_in.shape[-1]
    sends = 4 * (fsdp - 1) + ctx - 1
    anywhere, vmem = pl.BlockSpec(memory_space=pl.ANY), pl.BlockSpec(memory_space=pltpu.VMEM)
    shape = jax.ShapeDtypeStruct
    return pl.pallas_call(
        functools.partial(front_kernel, dp == 2),
        in_specs=[anywhere] * 4 + [vmem] * 3,
        out_specs=[vmem, anywhere, anywhere, anywhere, vmem, vmem, vmem, vmem],
        out_shape=[
            shape((fsdp,) + qkv_in.shape, BF16),
            shape((fsdp,) + out_in.shape, BF16),
            shape(gu_in.shape, BF16),
            shape((fsdp,) + cot_in.shape, BF16),
            shape((D, rows), BF16),
            shape((ctx, 2, KVW, rows), BF16),
            shape((D, rows), BF16),
            shape((KV_HEADS, GROUP, rows), F32),
        ],
        scratch_shapes=[
            pltpu.VMEM((columns, rows), F32),
            pltpu.SemaphoreType.DMA((4,)),
            pltpu.SemaphoreType.DMA((sends,)),
            pltpu.SemaphoreType.DMA((sends,)),
            pltpu.SemaphoreType.DMA((3 * (fsdp - 1),)),
            pltpu.SemaphoreType.DMA((3 * (fsdp - 1),)),
        ],
        compiler_params=pltpu.CompilerParams(
            collective_id=0, has_side_effects=True, vmem_limit_bytes=48 * 2**20
        ),
        cost_estimate=pl.CostEstimate(
            flops=10**9, bytes_accessed=10**8, transcendentals=10**6
        ),
    )(qkv_in, out_in, gu_in, cot_in, normed, cosine, sine)


def padded(array, axis, to):
    widths = [(0, 0)] * array.ndim
    widths[axis] = (0, to - array.shape[axis])
    return jnp.pad(array, widths)


def shards(tokens, positions, gain_attn, gain_mlp, w_qkv, w_out, w_gu, w_down, cotangent):
    rows = tokens.shape[1]
    fsdp, ctx, dp = lax.axis_size("fsdp"), lax.axis_size("ctx"), lax.axis_size("dp")
    part = FF // fsdp
    own = D // fsdp
    slim = D // (fsdp * ctx)
    half, wide_half = own // 2, -(-own // 2 // 128) * 128
    pad = -(-slim // 16) * 16
    inputs = tokens[0].astype(F32)
    cosine, sine = angles_of(positions[0])
    gu_cut = w_gu.reshape(2, half, 2, fsdp, part).transpose(3, 0, 1, 2, 4)
    gu_cut = gu_cut.reshape(fsdp, 2, half, 2 * part)
    normed = normalize(inputs, gain_attn).astype(BF16)
    normed_cut = padded(normed.reshape(rows, 2 * fsdp, half).transpose(1, 0, 2), 2, wide_half)
    qkv_all, out_all, gu_all, cot_all, queries, every_kv, attended, lse = front(
        padded(w_qkv.reshape(2, half, -1), 1, wide_half),
        padded(w_out.reshape(2, half, D), 1, wide_half),
        padded(gu_cut, 2, wide_half),
        cotangent[0],
        normed_cut,
        cosine,
        sine,
    )
    full_qkv = qkv_all[:, :, :half].reshape(D, -1)
    full_out = out_all[:, :, :half].reshape(D, D)
    gu_part = gu_all[:, :, :half].reshape(D, 2 * part)
    cot_all = cot_all.reshape(fsdp * rows, D)

    hidden = inputs + dot(attended, full_out, 0, 0)
    normed_two = normalize(hidden, gain_mlp).astype(BF16)
    (two_all,) = swap(1, (normed_two, "fsdp", True))
    two_all = two_all.reshape(fsdp * rows, D)
    gate_up = dot(two_all, gu_part, 1, 0)
    gate, up = gate_up[:, :part], gate_up[:, part:]
    activated, swish_back = jax.vjp(lambda a, b: jax.nn.silu(a) * b, gate, up)
    activated = activated.astype(BF16)
    grad_activated = dot(cot_all, w_down, 1, 1)
    grad_gate, grad_up = swish_back(grad_activated)
    grad_gate_up = jnp.concatenate([grad_gate, grad_up], axis=1).astype(BF16)
    two_part = dot(grad_gate_up, gu_part, 1, 1).astype(BF16).reshape(fsdp, rows, D)
    down_part = dot(activated, w_down, 1, 0).astype(BF16).reshape(fsdp, rows, D)
    grad_down = halves(dot(activated, cot_all, 0, 0).astype(BF16), dp)

    def spread(array):
        array = array.reshape(-1, fsdp * ctx, slim)
        return padded(array, 2, pad).reshape(-1, fsdp * ctx * pad)

    grad_gu = dot(spread(two_all), grad_gate_up, 0, 0).astype(BF16)
    if dp == 2:
        grad_gu = halves(grad_gu, dp)
        two_sum, gu_sum, down_grads = swap(
            2, (two_part, "fsdp", False), (grad_gu, "dp", False), (grad_down, "dp", False)
        )
        gu_cols = total_of(gu_sum).astype(BF16)
    else:
        two_sum, down_grads = swap(2, (two_part, "fsdp", False), (grad_down, "dp", False))
        gu_cols = grad_gu
    grad_two = total_of(two_sum)
    down_grads = total_of(down_grads).astype(BF16).reshape(ctx, part // ctx, D // dp)
    gu_cols = gu_cols.reshape(fsdp, ctx, pad, -1).transpose(1, 0, 2, 3)

    grad_rows = cotangent[0].astype(F32)
    _, norm_back_two = jax.vjp(normalize, hidden, gain_mlp)
    grad_hidden_part, grad_gain_mlp = norm_back_two(grad_two)
    grad_hidden = grad_rows + grad_hidden_part
    grad_attn = grad_hidden.astype(BF16)
    grad_attended = dot(full_out, grad_attn, 1, 1).astype(BF16)
    attended_wide = padded(attended.reshape(fsdp * ctx, slim, rows), 1, pad).reshape(-1, rows)
    grad_out = dot(attended_wide, grad_attn, 1, 0).astype(BF16)
    grad_queries, kv_grads = attention_backward(queries, every_kv, grad_attended, lse)
    kv_sum, down_sum, result_down = swap(
        3,
        (kv_grads.reshape(ctx, 2 * KVW, rows), "ctx", False),
        (down_part, "fsdp", False),
        (down_grads, "ctx", False),
    )
    own_kv = total_of(kv_sum)
    outputs = hidden + total_of(down_sum)
    grad_project = jnp.concatenate(
        [
            rotate(grad_queries, cosine, -sine),
            rotate(own_kv[:KVW], cosine, -sine),
            own_kv[KVW:],
        ],
        axis=0,
    ).astype(BF16)
    grad_normed = dot(grad_project, full_qkv, 0, 1)
    grad_qkv = dot(spread(normed), grad_project, 0, 1).astype(BF16)
    _, norm_back_one = jax.vjp(normalize, inputs, gain_attn)
    grad_input_part, grad_gain_attn = norm_back_one(grad_normed)
    grad_inputs = grad_hidden + grad_input_part

    gains = jnp.stack([grad_gain_attn, grad_gain_mlp]).reshape(2, fsdp, ctx, slim)
    gains = padded(padded(gains.transpose(1, 2, 0, 3), 2, 8), 3, 128)
    both = jnp.concatenate([halves(grad_qkv, dp), halves(grad_out, dp)], axis=2)
    both, gains = swap(4, (both, "dp", False), (gains, "dp", True))
    both = total_of(both).astype(BF16).reshape(fsdp, ctx * pad, -1)
    both, gains, gu_sum = swap(
        5, (both, "fsdp", False), (total_of(gains), "fsdp", False), (gu_cols, "ctx", False)
    )
    both = total_of(both).astype(BF16).reshape(ctx, pad, -1)
    both, gains, gu_rows = swap(
        6,
        (both, "ctx", False),
        (total_of(gains), "ctx", False),
        (total_of(gu_sum).astype(BF16), "fsdp", False),
    )
    both, gains = total_of(both)[:slim], total_of(gains)[:2, :slim]
    gu_rows = gu_rows[:, :slim]
    if dp == 2:
        result_gu = gu_rows.transpose(1, 0, 2).reshape(slim, FF)
    else:
        gu_rows = gu_rows.reshape(fsdp, slim, 2, part).transpose(1, 2, 0, 3).reshape(slim, 2 * FF)
        result_gu = lax.psum_scatter(gu_rows, "dp", scatter_dimension=1, tiled=True)
    wide = w_qkv.shape[1] // dp
    return (
        outputs[None],
        grad_inputs[None],
        gains[0],
        gains[1],
        both[:, :wide],
        both[:, wide:],
        result_gu.astype(F32),
        total_of(result_down),
    )


def total_of(array):
    return jnp.sum(array.astype(F32), axis=0)


def solution(mesh):
    placed = (
        P(("dp", "fsdp"), "ctx", None),
        P(("dp", "fsdp"), "ctx"),
        P(),
        P(),
        P("fsdp", None),
        P("fsdp", None),
        P("fsdp", None),
        P("fsdp", None),
        P(("dp", "fsdp"), "ctx", None),
    )
    return jax.shard_map(
        shards,
        mesh=mesh,
        in_specs=placed,
        out_specs=(
            P(("dp", "fsdp"), "ctx", None),
            P(("dp", "fsdp"), "ctx", None),
            P(("fsdp", "ctx")),
            P(("fsdp", "ctx")),
            P(("fsdp", "ctx"), "dp"),
            P(("fsdp", "ctx"), "dp"),
            P(("fsdp", "ctx"), "dp"),
            P(("fsdp", "ctx"), "dp"),
        ),
        check_vma=False,
    )
```

```python
import functools

import jax
import jax.numpy as jnp
from jax import lax
from jax.experimental import pallas as pl
from jax.experimental.pallas import tpu as pltpu
from jax.sharding import PartitionSpec as P

D = 960
HEADS = 15
KV_HEADS = 5
HD = 64
FF = 2560
GROUP = HEADS // KV_HEADS
KVW = KV_HEADS * HD
EPSILON = 1e-05
F32 = jnp.float32
BF16 = jnp.bfloat16


def dot(a, b, ca, cb):
    return lax.dot_general(a, b, (((ca,), (cb,)), ((), ())), preferred_element_type=F32)


def normalize(values, gain):
    return values * lax.rsqrt(jnp.mean(values * values, axis=-1, keepdims=True) + EPSILON) * gain


def angles_of(places):
    half = HD // 2
    frequency = 10000.0 ** (-jnp.arange(half, dtype=F32) / half)
    angles = frequency[:, None] * places.astype(F32)[None, :]
    return jnp.cos(angles), jnp.sin(angles)


def rotate(values, cosine, sine):
    length = values.shape[1]
    parts = values.reshape(-1, 2, HD // 2, length)
    front, back = parts[:, 0], parts[:, 1]
    turned = jnp.stack([front * cosine - back * sine, back * cosine + front * sine], axis=1)
    return turned.reshape(-1, length)


def keys_first(kv, which):
    pieces = [kv[c, which] for c in range(kv.shape[0])]
    return (
        jnp.concatenate([piece.T for piece in pieces], axis=0),
        jnp.concatenate(pieces, axis=1),
    )


def allowed_of(keys, rows):
    start = lax.axis_index("ctx") * rows
    key_at = lax.broadcasted_iota(jnp.int32, (keys, rows), 0)
    row_at = lax.broadcasted_iota(jnp.int32, (keys, rows), 1)
    return key_at <= row_at + start


def backward_kernel(q_ref, kv_ref, g_ref, lse_ref, dq_ref, dkv_ref):
    rows = q_ref.shape[1]
    kv = kv_ref[...]
    parts = kv.shape[0]
    keys, keys_t = keys_first(kv, 0)
    values, _ = keys_first(kv, 1)
    allowed = allowed_of(keys.shape[0], rows)
    dk = jnp.zeros((HD, keys.shape[0]), F32)
    dv = jnp.zeros((HD, keys.shape[0]), F32)
    for h in range(GROUP):
        q = q_ref[h * HD : (h + 1) * HD, :]
        g = g_ref[h * HD : (h + 1) * HD, :]
        scores = jnp.where(allowed, dot(keys, q, 1, 0), -1e30)
        prob = jnp.exp(scores - lse_ref[0, h : h + 1, :])
        dprob = dot(values, g, 1, 0)
        inner = jnp.sum(dprob * prob, axis=0, keepdims=True)
        ds = (prob * (dprob - inner)).astype(BF16)
        dq_ref[h * HD : (h + 1) * HD, :] = dot(keys_t, ds, 1, 0) * (HD**-0.5)
        dk = dk + dot(q, ds, 1, 1)
        dv = dv + dot(g, prob.astype(BF16), 1, 1)
    for c in range(parts):
        dkv_ref[c, 0] = dk[:, c * rows : (c + 1) * rows].astype(BF16)
        dkv_ref[c, 1] = dv[:, c * rows : (c + 1) * rows].astype(BF16)


def attention_specs(parts, rows):
    q_spec = pl.BlockSpec((GROUP * HD, rows), lambda g: (g, 0))
    kv_spec = pl.BlockSpec((parts, 2, HD, rows), lambda g: (0, 0, g, 0))
    lse_spec = pl.BlockSpec((1, GROUP, rows), lambda g: (g, 0, 0))
    return q_spec, kv_spec, lse_spec


def attention_backward(q, kv, g, lse):
    parts, rows = kv.shape[0], q.shape[1]
    q_spec, kv_spec, lse_spec = attention_specs(parts, rows)
    work = parts * rows * rows * HD * HEADS
    return pl.pallas_call(
        backward_kernel,
        grid=(KV_HEADS,),
        in_specs=[q_spec, kv_spec, q_spec, lse_spec],
        out_specs=[q_spec, kv_spec],
        out_shape=[
            jax.ShapeDtypeStruct((D, rows), F32),
            jax.ShapeDtypeStruct(kv.shape, BF16),
        ],
        compiler_params=pltpu.CompilerParams(vmem_limit_bytes=40 * 2**20),
        cost_estimate=pl.CostEstimate(
            flops=40 * work, bytes_accessed=5 * 2**20, transcendentals=work // HD
        ),
    )(q, kv, g, lse)


MESH = pl.DeviceIdType.MESH


def peer_of(axis, k):
    size = lax.axis_size(axis)
    return lax.rem(lax.axis_index(axis) + k, size)


def greet(axes):
    barrier = pltpu.get_barrier_semaphore()
    count = 0
    for axis in axes:
        for k in range(1, lax.axis_size(axis)):
            pl.semaphore_signal(
                barrier, inc=1, device_id={axis: peer_of(axis, k)}, device_id_type=MESH
            )
            count += 1
    pl.semaphore_wait(barrier, count)


def send(src, dst, sems, at, axis, k):
    copy = pltpu.make_async_remote_copy(
        src_ref=src,
        dst_ref=dst,
        send_sem=sems[0].at[at],
        recv_sem=sems[1].at[at],
        device_id={axis: peer_of(axis, k)},
        device_id_type=MESH,
    )
    copy.start()
    return copy


def swap_kernel(plan, *refs):
    count = len(plan)
    ins, outs = refs[:count], refs[count : 2 * count]
    send_sem, recv_sem = refs[2 * count :]
    greet(sorted({axis for axis, _ in plan}))
    copies, at = [], 0
    for i, (axis, kind) in enumerate(plan):
        me = lax.axis_index(axis)
        for k in range(1, lax.axis_size(axis)):
            there = peer_of(axis, k)
            if kind == "all":
                src = ins[i]
            elif kind == "rows":
                src = ins[i].at[there]
            else:
                width = outs[i].shape[-1]
                src = ins[i].at[:, pl.ds(pl.multiple_of(there * width, 128), width)]
            copies.append(send(src, outs[i].at[me], (send_sem, recv_sem), at, axis, k))
            at += 1
    for copy in copies:
        copy.wait()


def swap(collective_id, *items):
    plan = [(axis, kind) for _, axis, kind in items]

    def shape_of(x, axis, kind):
        size = lax.axis_size(axis)
        if kind == "all":
            return (size,) + x.shape
        if kind == "rows":
            return x.shape
        return (size, x.shape[0], x.shape[1] // size)

    shapes = [jax.ShapeDtypeStruct(shape_of(*item), item[0].dtype) for item in items]
    total = sum(lax.axis_size(axis) - 1 for axis, _ in plan)
    size = sum(shape.size * shape.dtype.itemsize for shape in shapes)
    return pl.pallas_call(
        functools.partial(swap_kernel, plan),
        in_specs=[pl.BlockSpec(memory_space=pl.ANY)] * len(plan),
        out_specs=[pl.BlockSpec(memory_space=pl.ANY)] * len(plan),
        out_shape=shapes,
        scratch_shapes=[
            pltpu.SemaphoreType.DMA((total,)),
            pltpu.SemaphoreType.DMA((total,)),
        ],
        compiler_params=pltpu.CompilerParams(collective_id=collective_id, has_side_effects=True),
        cost_estimate=pl.CostEstimate(flops=0, bytes_accessed=20 * size, transcendentals=0),
    )(*[x for x, _, _ in items])


def front_kernel(
    shared, qkv_in, out_in, gu_in, cot_in, normed, cosine, sine,
    qkv, out_all, gu_all, cot_all, q_ref, kv, att_ref, lse_ref,
    project, local_sem, send_sem, recv_sem, pass_send, pass_recv,
):
    fsdp, ctx = lax.axis_size("fsdp"), lax.axis_size("ctx")
    me, here = lax.axis_index("fsdp"), lax.axis_index("ctx")
    side = lax.axis_index("dp")
    rows = normed.shape[1]
    part = FF // fsdp

    def columns_of(place, device):
        return pl.ds(pl.multiple_of(place * FF + device * part, 128), part)

    def gu_block(place, k):
        columns = columns_of(place, peer_of("fsdp", k))
        mine = pl.ds(place * part, part)
        if shared:
            return gu_in.at[side, :, columns], gu_all.at[me, side, :, mine]
        return gu_in.at[:, :, columns], gu_all.at[me, :, :, mine]

    sems, pass_sems = (send_sem, recv_sem), (pass_send, pass_recv)
    greet(("fsdp", "ctx") + (("dp",) if shared else ()))
    locals_ = [
        pltpu.make_async_copy(qkv_in, qkv.at[me], local_sem.at[0]),
        pltpu.make_async_copy(out_in, out_all.at[me], local_sem.at[1]),
        pltpu.make_async_copy(cot_in, cot_all.at[me], local_sem.at[2]),
    ] + [
        pltpu.make_async_copy(
            gu_in.at[:, :, columns_of(place, me)],
            gu_all.at[me, :, :, place * part : (place + 1) * part],
            local_sem.at[3 + place],
        )
        for place in range(2)
    ]
    for copy in locals_:
        copy.start()
    halves_of = lambda ref: ref.at[side] if shared else ref
    peers = range(1, fsdp)
    first = [
        send(halves_of(qkv_in), halves_of(qkv.at[me]), sems, k - 1, "fsdp", k) for k in peers
    ]
    rest, passed = [], []

    def hand_over(ref, base, arrivals):
        for k, copy in zip(peers, arrivals):
            copy.wait_recv()
            if shared:
                block = ref.at[lax.rem(me - k + fsdp, fsdp), side]
                passed.append(send(block, block, pass_sems, base + k - 1, "dp", 1))

    hand_over(qkv, 0, first)
    base = fsdp - 1
    seconds = [
        send(halves_of(out_in), halves_of(out_all.at[me]), sems, base + k - 1, "fsdp", k)
        for k in peers
    ]
    thirds = [
        send(*gu_block(0, k), sems, 2 * base + k - 1, "fsdp", k) for k in peers
    ]
    fourths = [
        send(*gu_block(1, k), sems, 3 * base + k - 1, "fsdp", k) for k in peers
    ]
    lasts = [send(cot_in, cot_all.at[me], sems, 4 * base + k - 1, "fsdp", k) for k in peers]
    for copy in passed:
        copy.wait_recv()
    locals_[0].wait()
    blocks = 2 * fsdp
    total = jnp.zeros(project.shape[::-1], F32)
    for b in range(blocks):
        total = total + dot(normed[b], qkv[b // 2, b % 2], 1, 0)
    project[...] = total.T
    half = HD // 2
    cos, sin = cosine[...], sine[...]
    mine = kv.at[here]

    def turn(h, carry):
        start = pl.multiple_of(h * HD, HD)
        a = project[pl.ds(start, half), :]
        b = project[pl.ds(start + half, half), :]
        q_ref[pl.ds(start, HD), :] = (
            jnp.concatenate([a * cos - b * sin, b * cos + a * sin], axis=0) * (HD**-0.5)
        ).astype(BF16)
        return carry

    for h in range(KV_HEADS):
        at = D + h * HD
        a, b = project[at : at + half, :], project[at + half : at + HD, :]
        mine[0, h * HD : (h + 1) * HD, :] = jnp.concatenate(
            [a * cos - b * sin, b * cos + a * sin], axis=0
        ).astype(BF16)
    mine[1, :, :] = project[D + KVW :, :].astype(BF16)
    kvs = [
        send(mine, mine, sems, 5 * base + k - 1, "ctx", k) for k in range(1, ctx)
    ]
    lax.fori_loop(0, HEADS, turn, 0)
    hand_over(out_all, base, seconds)
    for copy in kvs:
        copy.wait()
    allowed = allowed_of(ctx * rows, rows)

    def attend(g, carry):
        at = pl.ds(pl.multiple_of(g * HD, HD), HD)
        keys = jnp.concatenate([kv[c, 0, at, :].T for c in range(ctx)], axis=0)
        values_t = jnp.concatenate([kv[c, 1, at, :] for c in range(ctx)], axis=1)
        for h in range(GROUP):
            spot = pl.ds(pl.multiple_of((g * GROUP + h) * HD, HD), HD)
            scores = jnp.where(allowed, dot(keys, q_ref[spot, :], 1, 0), -1e30)
            row_max = jnp.max(scores, axis=0, keepdims=True)
            exponent = jnp.exp(scores - row_max)
            sums = jnp.sum(exponent, axis=0, keepdims=True)
            att = dot(values_t, exponent.astype(BF16), 1, 0) / sums
            att_ref[spot, :] = att.astype(BF16)
            lse_ref[g, h : h + 1, :] = row_max + jnp.log(sums)
        return carry

    lax.fori_loop(0, KV_HEADS, attend, 0)
    for copy in fourths:
        copy.wait_recv()
    hand_over(gu_all, 2 * base, thirds)
    for copy in lasts:
        copy.wait_recv()
    for copy in first + seconds + thirds + fourths + lasts:
        copy.wait_send()
    for i, copy in enumerate(passed):
        copy.wait_send()
        if i >= base:
            copy.wait_recv()
    for copy in locals_[1:]:
        copy.wait()


def front(qkv_in, out_in, gu_in, cot_in, normed, cosine, sine):
    fsdp, ctx, dp = lax.axis_size("fsdp"), lax.axis_size("ctx"), lax.axis_size("dp")
    rows = normed.shape[1]
    columns = qkv_in.shape[-1]
    sends = 5 * (fsdp - 1) + ctx - 1
    anywhere, vmem = pl.BlockSpec(memory_space=pl.ANY), pl.BlockSpec(memory_space=pltpu.VMEM)
    shape = jax.ShapeDtypeStruct
    return pl.pallas_call(
        functools.partial(front_kernel, dp == 2),
        in_specs=[anywhere] * 4 + [vmem] * 3,
        out_specs=[vmem] * 8,
        out_shape=[
            shape((fsdp,) + qkv_in.shape, BF16),
            shape((fsdp,) + out_in.shape, BF16),
            shape((fsdp,) + gu_in.shape[:2] + (2 * FF // fsdp,), BF16),
            shape((fsdp,) + cot_in.shape, BF16),
            shape((D, rows), BF16),
            shape((ctx, 2, KVW, rows), BF16),
            shape((D, rows), BF16),
            shape((KV_HEADS, GROUP, rows), F32),
        ],
        scratch_shapes=[
            pltpu.VMEM((columns, rows), F32),
            pltpu.SemaphoreType.DMA((5,)),
            pltpu.SemaphoreType.DMA((sends,)),
            pltpu.SemaphoreType.DMA((sends,)),
            pltpu.SemaphoreType.DMA((3 * (fsdp - 1),)),
            pltpu.SemaphoreType.DMA((3 * (fsdp - 1),)),
        ],
        compiler_params=pltpu.CompilerParams(
            collective_id=0, has_side_effects=True, vmem_limit_bytes=48 * 2**20
        ),
        cost_estimate=pl.CostEstimate(
            flops=10**9, bytes_accessed=10**8, transcendentals=10**6
        ),
    )(qkv_in, out_in, gu_in, cot_in, normed, cosine, sine)


def padded(array, axis, to):
    widths = [(0, 0)] * array.ndim
    widths[axis] = (0, to - array.shape[axis])
    return jnp.pad(array, widths)


def shards(tokens, positions, gain_attn, gain_mlp, w_qkv, w_out, w_gu, w_down, cotangent):
    rows = tokens.shape[1]
    fsdp, ctx, dp = lax.axis_size("fsdp"), lax.axis_size("ctx"), lax.axis_size("dp")
    part = FF // fsdp
    own = D // fsdp
    slim = D // (fsdp * ctx)
    half, wide_half = own // 2, -(-own // 2 // 128) * 128
    pad = -(-slim // 16) * 16
    inputs = tokens[0].astype(F32)
    cosine, sine = angles_of(positions[0])
    normed = normalize(inputs, gain_attn).astype(BF16)
    normed_cut = padded(normed.reshape(rows, 2 * fsdp, half).transpose(1, 0, 2), 2, wide_half)
    qkv_all, out_all, gu_all, cot_all, queries, every_kv, attended, lse = front(
        padded(w_qkv.reshape(2, half, -1), 1, wide_half),
        padded(w_out.reshape(2, half, D), 1, wide_half),
        padded(w_gu.reshape(2, half, 2 * FF), 1, wide_half),
        cotangent[0],
        normed_cut,
        cosine,
        sine,
    )
    full_qkv = qkv_all[:, :, :half].reshape(D, -1)
    full_out = out_all[:, :, :half].reshape(D, D)
    gu_part = gu_all[:, :, :half].reshape(D, 2 * part)
    cot_all = cot_all.reshape(fsdp * rows, D)

    hidden = inputs + dot(attended, full_out, 0, 0)
    normed_two = normalize(hidden, gain_mlp).astype(BF16)
    (two_all,) = swap(1, (normed_two, "fsdp", "all"))
    two_all = with_own(two_all, normed_two, "fsdp").reshape(fsdp * rows, D)
    gate_up = dot(two_all, gu_part, 1, 0)
    gate, up = gate_up[:, :part], gate_up[:, part:]
    activated, swish_back = jax.vjp(lambda a, b: jax.nn.silu(a) * b, gate, up)
    activated = activated.astype(BF16)
    grad_activated = dot(cot_all, w_down, 1, 1)
    grad_gate, grad_up = swish_back(grad_activated)
    grad_gate_up = jnp.concatenate([grad_gate, grad_up], axis=1).astype(BF16)
    two_part = dot(grad_gate_up, gu_part, 1, 1).astype(BF16).reshape(fsdp, rows, D)
    down_part = dot(activated, w_down, 1, 0).astype(BF16).reshape(fsdp, rows, D)
    grad_down = dot(activated, in_halves(cot_all, 1, dp), 0, 0).astype(BF16)

    def spread(array):
        array = array.reshape(-1, fsdp * ctx, slim)
        return padded(array, 2, pad).reshape(-1, fsdp * ctx * pad)

    grad_gu = dot(spread(two_all), grad_gate_up, 0, 0).astype(BF16)
    if dp == 2:
        two_sum, down_grads, gu_sum = swap(
            2,
            (two_part, "fsdp", "rows"),
            (grad_down, "dp", "columns"),
            (grad_gu, "dp", "columns"),
        )
        gu_cols = total_of(gu_sum, grad_gu, "dp", "columns").astype(BF16)
    else:
        two_sum, down_grads = swap(2, (two_part, "fsdp", "rows"), (grad_down, "dp", "columns"))
        gu_cols = grad_gu
    grad_two = total_of(two_sum, two_part, "fsdp", "rows")
    down_grads = total_of(down_grads, grad_down, "dp", "columns").astype(BF16)
    down_grads = down_grads.reshape(ctx, part // ctx, -1)
    gu_cols = gu_cols.reshape(fsdp, ctx, pad, -1).transpose(1, 0, 2, 3)

    grad_rows = cotangent[0].astype(F32)
    _, norm_back_two = jax.vjp(normalize, hidden, gain_mlp)
    grad_hidden_part, grad_gain_mlp = norm_back_two(grad_two)
    grad_hidden = grad_rows + grad_hidden_part
    grad_attn = grad_hidden.astype(BF16)
    grad_attended = dot(full_out, grad_attn, 1, 1).astype(BF16)
    attended_wide = padded(attended.reshape(fsdp * ctx, slim, rows), 1, pad).reshape(-1, rows)
    grad_out = dot(attended_wide, in_halves(grad_attn, 1, dp), 1, 0).astype(BF16)
    grad_queries, kv_grads = attention_backward(queries, every_kv, grad_attended, lse)
    kv_grads = kv_grads.reshape(ctx, 2 * KVW, rows)
    kv_sum, down_sum, last_down = swap(
        3, (kv_grads, "ctx", "rows"), (down_part, "fsdp", "rows"), (down_grads, "ctx", "rows")
    )
    own_kv = total_of(kv_sum, kv_grads, "ctx", "rows")
    outputs = hidden + total_of(down_sum, down_part, "fsdp", "rows")
    result_down = total_of(last_down, down_grads, "ctx", "rows")[:, : D // dp]
    grad_project = jnp.concatenate(
        [
            rotate(grad_queries, cosine, -sine),
            rotate(own_kv[:KVW], cosine, -sine),
            own_kv[KVW:],
        ],
        axis=0,
    ).astype(BF16)
    grad_normed = dot(grad_project, full_qkv, 0, 1)
    grad_qkv = dot(spread(normed), in_halves(grad_project, 0, dp), 0, 1).astype(BF16)
    _, norm_back_one = jax.vjp(normalize, inputs, gain_attn)
    grad_input_part, grad_gain_attn = norm_back_one(grad_normed)
    grad_inputs = grad_hidden + grad_input_part

    gains = jnp.stack([grad_gain_attn, grad_gain_mlp]).reshape(2, fsdp, ctx, slim)
    gains = padded(padded(gains.transpose(1, 2, 0, 3), 2, 8), 3, 128)
    arrived = swap(4, (grad_qkv, "dp", "columns"), (grad_out, "dp", "columns"), (gains, "dp", "all"))
    sent = [
        total_of(arrived[0], grad_qkv, "dp", "columns").astype(BF16).reshape(fsdp, ctx * pad, -1),
        total_of(arrived[1], grad_out, "dp", "columns").astype(BF16).reshape(fsdp, ctx * pad, -1),
        total_of(arrived[2], gains, "dp", "all"),
        gu_cols,
    ]
    arrived = swap(
        5, *[(x, axis, "rows") for x, axis in zip(sent, ("fsdp", "fsdp", "fsdp", "ctx"))]
    )
    sent = [
        total_of(arrived[0], sent[0], "fsdp", "rows").astype(BF16).reshape(ctx, pad, -1),
        total_of(arrived[1], sent[1], "fsdp", "rows").astype(BF16).reshape(ctx, pad, -1),
        total_of(arrived[2], sent[2], "fsdp", "rows"),
        total_of(arrived[3], sent[3], "ctx", "rows").astype(BF16),
    ]
    arrived = swap(
        6, *[(x, axis, "rows") for x, axis in zip(sent, ("ctx", "ctx", "ctx", "fsdp"))]
    )
    result_qkv, result_out, gains = [
        total_of(arrived[i], sent[i], "ctx", "rows") for i in range(3)
    ]
    gains = gains[:2, :slim]
    own_gu = lax.dynamic_index_in_dim(sent[3], lax.axis_index("fsdp"), 0, keepdims=False)
    gu_rows = with_own(arrived[3], own_gu, "fsdp")
    gu_rows = gu_rows[:, :slim]
    if dp == 2:
        result_gu = gu_rows.transpose(1, 0, 2).reshape(slim, FF)
    else:
        gu_rows = gu_rows.reshape(fsdp, slim, 2, part).transpose(1, 2, 0, 3).reshape(slim, 2 * FF)
        result_gu = lax.psum_scatter(gu_rows, "dp", scatter_dimension=1, tiled=True)
    return (
        outputs[None],
        grad_inputs[None],
        gains[0],
        gains[1],
        result_qkv[:slim, : w_qkv.shape[1] // dp],
        result_out[:slim, : D // dp],
        result_gu.astype(F32),
        result_down,
    )


def total_of(received, sent, axis, kind):
    me, size = lax.axis_index(axis), lax.axis_size(axis)
    if kind == "all":
        own = sent
    elif kind == "rows":
        own = lax.dynamic_index_in_dim(sent, me, 0, keepdims=False)
    else:
        width = received.shape[-1]
        own = lax.dynamic_slice_in_dim(sent, me * width, width, 1)
    total = own.astype(F32)
    for j in range(size):
        total = total + jnp.where(me == j, 0.0, received[j].astype(F32))
    return total


def with_own(received, own, axis):
    return lax.dynamic_update_index_in_dim(received, own, lax.axis_index(axis), 0)


def in_halves(array, axis, count):
    size = array.shape[axis] // count
    to = -(-size // 128) * 128
    shape = array.shape[:axis] + (count, size) + array.shape[axis + 1 :]
    flat = array.shape[:axis] + (count * to,) + array.shape[axis + 1 :]
    return padded(array.reshape(shape), axis + 1, to).reshape(flat)


def solution(mesh):
    placed = (
        P(("dp", "fsdp"), "ctx", None),
        P(("dp", "fsdp"), "ctx"),
        P(),
        P(),
        P("fsdp", None),
        P("fsdp", None),
        P("fsdp", None),
        P("fsdp", None),
        P(("dp", "fsdp"), "ctx", None),
    )
    return jax.shard_map(
        shards,
        mesh=mesh,
        in_specs=placed,
        out_specs=(
            P(("dp", "fsdp"), "ctx", None),
            P(("dp", "fsdp"), "ctx", None),
            P(("fsdp", "ctx")),
            P(("fsdp", "ctx")),
            P(("fsdp", "ctx"), "dp"),
            P(("fsdp", "ctx"), "dp"),
            P(("fsdp", "ctx"), "dp"),
            P(("fsdp", "ctx"), "dp"),
        ),
        check_vma=False,
    )
```

```python
import functools

import jax
import jax.numpy as jnp
from jax import lax
from jax.experimental import pallas as pl
from jax.experimental.pallas import tpu as pltpu
from jax.sharding import PartitionSpec as P

D = 960
HEADS = 15
KV_HEADS = 5
HD = 64
FF = 2560
GROUP = HEADS // KV_HEADS
KVW = KV_HEADS * HD
EPSILON = 1e-05
F32 = jnp.float32
BF16 = jnp.bfloat16


def dot(a, b, ca, cb):
    return lax.dot_general(a, b, (((ca,), (cb,)), ((), ())), preferred_element_type=F32)


def normalize(values, gain):
    return values * lax.rsqrt(jnp.mean(values * values, axis=-1, keepdims=True) + EPSILON) * gain


def angles_of(places):
    half = HD // 2
    frequency = 10000.0 ** (-jnp.arange(half, dtype=F32) / half)
    angles = frequency[:, None] * places.astype(F32)[None, :]
    return jnp.cos(angles), jnp.sin(angles)


def rotate(values, cosine, sine):
    length = values.shape[1]
    parts = values.reshape(-1, 2, HD // 2, length)
    front, back = parts[:, 0], parts[:, 1]
    turned = jnp.stack([front * cosine - back * sine, back * cosine + front * sine], axis=1)
    return turned.reshape(-1, length)


def keys_first(kv, which):
    pieces = [kv[c, which] for c in range(kv.shape[0])]
    return (
        jnp.concatenate([piece.T for piece in pieces], axis=0),
        jnp.concatenate(pieces, axis=1),
    )


def allowed_of(keys, rows):
    start = lax.axis_index("ctx") * rows
    key_at = lax.broadcasted_iota(jnp.int32, (keys, rows), 0)
    row_at = lax.broadcasted_iota(jnp.int32, (keys, rows), 1)
    return key_at <= row_at + start


MESH = pl.DeviceIdType.MESH


def peer_of(axis, k):
    size = lax.axis_size(axis)
    return lax.rem(lax.axis_index(axis) + k, size)


def greet(axes):
    barrier = pltpu.get_barrier_semaphore()
    count = 0
    for axis in axes:
        for k in range(1, lax.axis_size(axis)):
            pl.semaphore_signal(
                barrier, inc=1, device_id={axis: peer_of(axis, k)}, device_id_type=MESH
            )
            count += 1
    pl.semaphore_wait(barrier, count)


def send(src, dst, sems, at, axis, k):
    copy = pltpu.make_async_remote_copy(
        src_ref=src,
        dst_ref=dst,
        send_sem=sems[0].at[at],
        recv_sem=sems[1].at[at],
        device_id={axis: peer_of(axis, k)},
        device_id_type=MESH,
    )
    copy.start()
    return copy


def swap_kernel(plan, *refs):
    count = len(plan)
    ins, outs = refs[:count], refs[count : 2 * count]
    send_sem, recv_sem = refs[2 * count :]
    greet(sorted({axis for axis, _ in plan}))
    copies, at = [], 0
    for i, (axis, kind) in enumerate(plan):
        me = lax.axis_index(axis)
        for k in range(1, lax.axis_size(axis)):
            there = peer_of(axis, k)
            if kind == "all":
                src = ins[i]
            elif kind == "rows":
                src = ins[i].at[there]
            else:
                width = outs[i].shape[-1]
                src = ins[i].at[:, pl.ds(pl.multiple_of(there * width, 128), width)]
            copies.append(send(src, outs[i].at[me], (send_sem, recv_sem), at, axis, k))
            at += 1
    for copy in copies:
        copy.wait()


def swap(collective_id, *items):
    plan = [(axis, kind) for _, axis, kind in items]

    def shape_of(x, axis, kind):
        size = lax.axis_size(axis)
        if kind == "all":
            return (size,) + x.shape
        if kind == "rows":
            return x.shape
        return (size, x.shape[0], x.shape[1] // size)

    shapes = [jax.ShapeDtypeStruct(shape_of(*item), item[0].dtype) for item in items]
    total = sum(lax.axis_size(axis) - 1 for axis, _ in plan)
    size = sum(shape.size * shape.dtype.itemsize for shape in shapes)
    return pl.pallas_call(
        functools.partial(swap_kernel, plan),
        in_specs=[pl.BlockSpec(memory_space=pl.ANY)] * len(plan),
        out_specs=[pl.BlockSpec(memory_space=pl.ANY)] * len(plan),
        out_shape=shapes,
        scratch_shapes=[
            pltpu.SemaphoreType.DMA((total,)),
            pltpu.SemaphoreType.DMA((total,)),
        ],
        compiler_params=pltpu.CompilerParams(collective_id=collective_id, has_side_effects=True),
        cost_estimate=pl.CostEstimate(flops=0, bytes_accessed=20 * size, transcendentals=0),
    )(*[x for x, _, _ in items])


def front_kernel(
    shared, qkv_in, out_in, gu_in, cot_in, normed, cosine, sine,
    qkv, out_all, gu_all, cot_all, q_ref, kv, att_ref, lse_ref,
    project, local_sem, send_sem, recv_sem, pass_send, pass_recv,
):
    fsdp, ctx = lax.axis_size("fsdp"), lax.axis_size("ctx")
    me, here = lax.axis_index("fsdp"), lax.axis_index("ctx")
    side = lax.axis_index("dp")
    rows = normed.shape[1]
    part = FF // fsdp

    def columns_of(place, device):
        return pl.ds(pl.multiple_of(place * FF + device * part, 128), part)

    def gu_block(place, k):
        columns = columns_of(place, peer_of("fsdp", k))
        mine = pl.ds(place * part, part)
        if shared:
            return gu_in.at[side, :, columns], gu_all.at[me, side, :, mine]
        return gu_in.at[:, :, columns], gu_all.at[me, :, :, mine]

    sems, pass_sems = (send_sem, recv_sem), (pass_send, pass_recv)
    greet(("fsdp", "ctx") + (("dp",) if shared else ()))
    locals_ = [
        pltpu.make_async_copy(qkv_in, qkv.at[me], local_sem.at[0]),
        pltpu.make_async_copy(out_in, out_all.at[me], local_sem.at[1]),
        pltpu.make_async_copy(cot_in, cot_all.at[me], local_sem.at[2]),
    ] + [
        pltpu.make_async_copy(
            gu_in.at[:, :, columns_of(place, me)],
            gu_all.at[me, :, :, place * part : (place + 1) * part],
            local_sem.at[3 + place],
        )
        for place in range(2)
    ]
    for copy in locals_:
        copy.start()
    halves_of = lambda ref: ref.at[side] if shared else ref
    peers = range(1, fsdp)
    first = [
        send(halves_of(qkv_in), halves_of(qkv.at[me]), sems, k - 1, "fsdp", k) for k in peers
    ]
    rest, passed = [], []

    def hand_over(ref, base, arrivals):
        for k, copy in zip(peers, arrivals):
            copy.wait_recv()
            if shared:
                block = ref.at[lax.rem(me - k + fsdp, fsdp), side]
                passed.append(send(block, block, pass_sems, base + k - 1, "dp", 1))

    hand_over(qkv, 0, first)
    base = fsdp - 1
    seconds = [
        send(halves_of(out_in), halves_of(out_all.at[me]), sems, base + k - 1, "fsdp", k)
        for k in peers
    ]
    thirds = [
        send(*gu_block(0, k), sems, 2 * base + k - 1, "fsdp", k) for k in peers
    ]
    fourths = [
        send(*gu_block(1, k), sems, 3 * base + k - 1, "fsdp", k) for k in peers
    ]
    lasts = [send(cot_in, cot_all.at[me], sems, 4 * base + k - 1, "fsdp", k) for k in peers]
    for copy in passed:
        copy.wait_recv()
    locals_[0].wait()
    blocks = 2 * fsdp
    total = jnp.zeros(project.shape[::-1], F32)
    for b in range(blocks):
        total = total + dot(normed[b], qkv[b // 2, b % 2], 1, 0)
    project[...] = total.T
    half = HD // 2
    cos, sin = cosine[...], sine[...]
    mine = kv.at[here]

    def turn(h, carry):
        start = pl.multiple_of(h * HD, HD)
        a = project[pl.ds(start, half), :]
        b = project[pl.ds(start + half, half), :]
        q_ref[pl.ds(start, HD), :] = (
            jnp.concatenate([a * cos - b * sin, b * cos + a * sin], axis=0) * (HD**-0.5)
        ).astype(BF16)
        return carry

    for h in range(KV_HEADS):
        at = D + h * HD
        a, b = project[at : at + half, :], project[at + half : at + HD, :]
        mine[0, h * HD : (h + 1) * HD, :] = jnp.concatenate(
            [a * cos - b * sin, b * cos + a * sin], axis=0
        ).astype(BF16)
    mine[1, :, :] = project[D + KVW :, :].astype(BF16)
    kvs = [
        send(mine, mine, sems, 5 * base + k - 1, "ctx", k) for k in range(1, ctx)
    ]
    lax.fori_loop(0, HEADS, turn, 0)
    hand_over(out_all, base, seconds)
    for copy in kvs:
        copy.wait()
    allowed = allowed_of(ctx * rows, rows)

    def attend(g, carry):
        at = pl.ds(pl.multiple_of(g * HD, HD), HD)
        keys = jnp.concatenate([kv[c, 0, at, :].T for c in range(ctx)], axis=0)
        values_t = jnp.concatenate([kv[c, 1, at, :] for c in range(ctx)], axis=1)
        for h in range(GROUP):
            spot = pl.ds(pl.multiple_of((g * GROUP + h) * HD, HD), HD)
            scores = jnp.where(allowed, dot(keys, q_ref[spot, :], 1, 0), -1e30)
            row_max = jnp.max(scores, axis=0, keepdims=True)
            exponent = jnp.exp(scores - row_max)
            sums = jnp.sum(exponent, axis=0, keepdims=True)
            att = dot(values_t, exponent.astype(BF16), 1, 0) / sums
            att_ref[spot, :] = att.astype(BF16)
            lse_ref[g, h : h + 1, :] = row_max + jnp.log(sums)
        return carry

    lax.fori_loop(0, KV_HEADS, attend, 0)
    for copy in fourths:
        copy.wait_recv()
    hand_over(gu_all, 2 * base, thirds)
    for copy in lasts:
        copy.wait_recv()
    for copy in first + seconds + thirds + fourths + lasts:
        copy.wait_send()
    for i, copy in enumerate(passed):
        copy.wait_send()
        if i >= base:
            copy.wait_recv()
    for copy in locals_[1:]:
        copy.wait()


def front(qkv_in, out_in, gu_in, cot_in, normed, cosine, sine):
    fsdp, ctx, dp = lax.axis_size("fsdp"), lax.axis_size("ctx"), lax.axis_size("dp")
    rows = normed.shape[1]
    columns = qkv_in.shape[-1]
    sends = 5 * (fsdp - 1) + ctx - 1
    anywhere, vmem = pl.BlockSpec(memory_space=pl.ANY), pl.BlockSpec(memory_space=pltpu.VMEM)
    shape = jax.ShapeDtypeStruct
    return pl.pallas_call(
        functools.partial(front_kernel, dp == 2),
        in_specs=[anywhere] * 4 + [vmem] * 3,
        out_specs=[vmem] * 8,
        out_shape=[
            shape((fsdp,) + qkv_in.shape, BF16),
            shape((fsdp,) + out_in.shape, BF16),
            shape((fsdp,) + gu_in.shape[:2] + (2 * FF // fsdp,), BF16),
            shape((fsdp,) + cot_in.shape, BF16),
            shape((D, rows), BF16),
            shape((ctx, 2, KVW, rows), BF16),
            shape((D, rows), BF16),
            shape((KV_HEADS, GROUP, rows), F32),
        ],
        scratch_shapes=[
            pltpu.VMEM((columns, rows), F32),
            pltpu.SemaphoreType.DMA((5,)),
            pltpu.SemaphoreType.DMA((sends,)),
            pltpu.SemaphoreType.DMA((sends,)),
            pltpu.SemaphoreType.DMA((3 * (fsdp - 1),)),
            pltpu.SemaphoreType.DMA((3 * (fsdp - 1),)),
        ],
        compiler_params=pltpu.CompilerParams(
            collective_id=0, has_side_effects=True, vmem_limit_bytes=48 * 2**20
        ),
        cost_estimate=pl.CostEstimate(
            flops=10**9, bytes_accessed=10**8, transcendentals=10**6
        ),
    )(qkv_in, out_in, gu_in, cot_in, normed, cosine, sine)


def back_kernel(
    q_ref, kv, g_ref, lse_ref, down_in, dq_ref, dkv, kv_out, down_out,
    down_send, down_recv, kv_send, kv_recv,
):
    fsdp, ctx = lax.axis_size("fsdp"), lax.axis_size("ctx")
    me, here = lax.axis_index("fsdp"), lax.axis_index("ctx")
    rows = q_ref.shape[1]
    greet(("fsdp", "ctx"))
    downs = [
        send(
            down_in.at[peer_of("fsdp", k)], down_out.at[me], (down_send, down_recv), k - 1, "fsdp", k
        )
        for k in range(1, fsdp)
    ]
    allowed = allowed_of(ctx * rows, rows)

    def kv_copy(g, k):
        at = pl.ds(pl.multiple_of(g * HD, HD), HD)
        spot = g * (ctx - 1) + k - 1
        there = peer_of("ctx", k)
        return pltpu.make_async_remote_copy(
            src_ref=dkv.at[there, :, at, :],
            dst_ref=kv_out.at[here, :, at, :],
            send_sem=kv_send.at[spot],
            recv_sem=kv_recv.at[spot],
            device_id={"ctx": there},
            device_id_type=MESH,
        )

    def attend_back(g, carry):
        at = pl.ds(pl.multiple_of(g * HD, HD), HD)
        keys = jnp.concatenate([kv[c, 0, at, :].T for c in range(ctx)], axis=0)
        keys_t = jnp.concatenate([kv[c, 0, at, :] for c in range(ctx)], axis=1)
        values = jnp.concatenate([kv[c, 1, at, :].T for c in range(ctx)], axis=0)
        dk = jnp.zeros((HD, ctx * rows), F32)
        dv = jnp.zeros((HD, ctx * rows), F32)
        for h in range(GROUP):
            spot = pl.ds(pl.multiple_of((g * GROUP + h) * HD, HD), HD)
            q, grad = q_ref[spot, :], g_ref[spot, :]
            scores = jnp.where(allowed, dot(keys, q, 1, 0), -1e30)
            prob = jnp.exp(scores - lse_ref[g, h : h + 1, :])
            dprob = dot(values, grad, 1, 0)
            inner = jnp.sum(dprob * prob, axis=0, keepdims=True)
            ds = (prob * (dprob - inner)).astype(BF16)
            dq_ref[spot, :] = dot(keys_t, ds, 1, 0) * (HD**-0.5)
            dk = dk + dot(q, ds, 1, 1)
            dv = dv + dot(grad, prob.astype(BF16), 1, 1)
        for c in range(ctx):
            dkv[c, 0, at, :] = dk[:, c * rows : (c + 1) * rows].astype(BF16)
            dkv[c, 1, at, :] = dv[:, c * rows : (c + 1) * rows].astype(BF16)
        for k in range(1, ctx):
            kv_copy(g, k).start()
        return carry

    def finish(g, carry):
        for k in range(1, ctx):
            kv_copy(g, k).wait()
        return carry

    lax.fori_loop(0, KV_HEADS, attend_back, 0)
    lax.fori_loop(0, KV_HEADS, finish, 0)
    for copy in downs:
        copy.wait()


def back(q, kv, g, lse, down_part):
    parts, rows = kv.shape[0], q.shape[1]
    fsdp = down_part.shape[0]
    work = parts * rows * rows * HD * HEADS
    anywhere, vmem = pl.BlockSpec(memory_space=pl.ANY), pl.BlockSpec(memory_space=pltpu.VMEM)
    shape = jax.ShapeDtypeStruct
    return pl.pallas_call(
        back_kernel,
        in_specs=[vmem] * 4 + [anywhere],
        out_specs=[vmem] * 3 + [anywhere],
        out_shape=[
            shape((D, rows), F32),
            shape(kv.shape, BF16),
            shape(kv.shape, BF16),
            shape(down_part.shape, BF16),
        ],
        scratch_shapes=[
            pltpu.SemaphoreType.DMA((fsdp - 1,)),
            pltpu.SemaphoreType.DMA((fsdp - 1,)),
            pltpu.SemaphoreType.DMA((KV_HEADS * (parts - 1),)),
            pltpu.SemaphoreType.DMA((KV_HEADS * (parts - 1),)),
        ],
        compiler_params=pltpu.CompilerParams(
            collective_id=3, has_side_effects=True, vmem_limit_bytes=48 * 2**20
        ),
        cost_estimate=pl.CostEstimate(
            flops=40 * work, bytes_accessed=5 * 2**20, transcendentals=work // HD
        ),
    )(q, kv, g, lse, down_part)


def padded(array, axis, to):
    widths = [(0, 0)] * array.ndim
    widths[axis] = (0, to - array.shape[axis])
    return jnp.pad(array, widths)


def shards(tokens, positions, gain_attn, gain_mlp, w_qkv, w_out, w_gu, w_down, cotangent):
    rows = tokens.shape[1]
    fsdp, ctx, dp = lax.axis_size("fsdp"), lax.axis_size("ctx"), lax.axis_size("dp")
    part = FF // fsdp
    own = D // fsdp
    slim = D // (fsdp * ctx)
    half, wide_half = own // 2, -(-own // 2 // 128) * 128
    pad = -(-slim // 16) * 16
    inputs = tokens[0].astype(F32)
    cosine, sine = angles_of(positions[0])
    normed = normalize(inputs, gain_attn).astype(BF16)
    normed_cut = padded(normed.reshape(rows, 2 * fsdp, half).transpose(1, 0, 2), 2, wide_half)
    qkv_all, out_all, gu_all, cot_all, queries, every_kv, attended, lse = front(
        padded(w_qkv.reshape(2, half, -1), 1, wide_half),
        padded(w_out.reshape(2, half, D), 1, wide_half),
        padded(w_gu.reshape(2, half, 2 * FF), 1, wide_half),
        cotangent[0],
        normed_cut,
        cosine,
        sine,
    )
    full_qkv = qkv_all[:, :, :half].reshape(D, -1)
    full_out = out_all[:, :, :half].reshape(D, D)
    gu_part = gu_all[:, :, :half].reshape(D, 2 * part)
    cot_all = cot_all.reshape(fsdp * rows, D)

    hidden = inputs + dot(attended, full_out, 0, 0)
    normed_two = normalize(hidden, gain_mlp).astype(BF16)
    (two_all,) = swap(1, (normed_two, "fsdp", "all"))
    two_all = with_own(two_all, normed_two, "fsdp").reshape(fsdp * rows, D)
    gate_up = dot(two_all, gu_part, 1, 0)
    gate, up = gate_up[:, :part], gate_up[:, part:]
    activated, swish_back = jax.vjp(lambda a, b: jax.nn.silu(a) * b, gate, up)
    activated = activated.astype(BF16)
    grad_activated = dot(cot_all, w_down, 1, 1)
    grad_gate, grad_up = swish_back(grad_activated)
    grad_gate_up = jnp.concatenate([grad_gate, grad_up], axis=1).astype(BF16)
    two_part = dot(grad_gate_up, gu_part, 1, 1).astype(BF16).reshape(fsdp, rows, D)
    down_part = dot(activated, w_down, 1, 0).astype(BF16).reshape(fsdp, rows, D)
    grad_down = dot(activated, in_halves(cot_all, 1, dp), 0, 0).astype(BF16)

    def spread(array):
        array = array.reshape(-1, fsdp * ctx, slim)
        return padded(array, 2, pad).reshape(-1, fsdp * ctx * pad)

    grad_gu = dot(spread(two_all), grad_gate_up, 0, 0).astype(BF16)
    grad_down = grad_down.reshape(ctx, part // ctx, -1)
    if dp == 2:
        two_sum, down_grads, gu_sum = swap(
            2, (two_part, "fsdp", "rows"), (grad_down, "ctx", "rows"), (grad_gu, "dp", "columns")
        )
        gu_cols = total_of(gu_sum, grad_gu, "dp", "columns").astype(BF16)
    else:
        two_sum, down_grads = swap(2, (two_part, "fsdp", "rows"), (grad_down, "ctx", "rows"))
        gu_cols = grad_gu
    grad_two = total_of(two_sum, two_part, "fsdp", "rows")
    down_grads = total_of(down_grads, grad_down, "ctx", "rows").astype(BF16)
    gu_cols = gu_cols.reshape(fsdp, ctx, pad, -1).transpose(1, 0, 2, 3)

    grad_rows = cotangent[0].astype(F32)
    _, norm_back_two = jax.vjp(normalize, hidden, gain_mlp)
    grad_hidden_part, grad_gain_mlp = norm_back_two(grad_two)
    grad_hidden = grad_rows + grad_hidden_part
    grad_attn = grad_hidden.astype(BF16)
    grad_attended = dot(full_out, grad_attn, 1, 1).astype(BF16)
    attended_wide = padded(attended.reshape(fsdp * ctx, slim, rows), 1, pad).reshape(-1, rows)
    grad_out = dot(attended_wide, in_halves(grad_attn, 1, dp), 1, 0).astype(BF16)
    grad_queries, kv_grads, kv_sum, down_sum = back(
        queries, every_kv, grad_attended, lse, down_part
    )
    own_kv = total_of(kv_sum, kv_grads, "ctx", "rows").reshape(2 * KVW, rows)
    outputs = hidden + total_of(down_sum, down_part, "fsdp", "rows")
    grad_project = jnp.concatenate(
        [
            rotate(grad_queries, cosine, -sine),
            rotate(own_kv[:KVW], cosine, -sine),
            own_kv[KVW:],
        ],
        axis=0,
    ).astype(BF16)
    grad_normed = dot(grad_project, full_qkv, 0, 1)
    grad_qkv = dot(spread(normed), in_halves(grad_project, 0, dp), 0, 1).astype(BF16)
    _, norm_back_one = jax.vjp(normalize, inputs, gain_attn)
    grad_input_part, grad_gain_attn = norm_back_one(grad_normed)
    grad_inputs = grad_hidden + grad_input_part

    gains = jnp.stack([grad_gain_attn, grad_gain_mlp]).reshape(2, fsdp, ctx, slim)
    gains = padded(padded(gains.transpose(1, 2, 0, 3), 2, 8), 3, 128)
    arrived = swap(
        4,
        (grad_qkv, "dp", "columns"),
        (grad_out, "dp", "columns"),
        (gains, "dp", "all"),
        (down_grads, "dp", "columns"),
    )
    result_down = total_of(arrived[3], down_grads, "dp", "columns")[:, : D // dp]
    sent = [
        total_of(arrived[0], grad_qkv, "dp", "columns").astype(BF16).reshape(fsdp, ctx * pad, -1),
        total_of(arrived[1], grad_out, "dp", "columns").astype(BF16).reshape(fsdp, ctx * pad, -1),
        total_of(arrived[2], gains, "dp", "all"),
        gu_cols,
    ]
    arrived = swap(
        5, *[(x, axis, "rows") for x, axis in zip(sent, ("fsdp", "fsdp", "fsdp", "ctx"))]
    )
    sent = [
        total_of(arrived[0], sent[0], "fsdp", "rows").astype(BF16).reshape(ctx, pad, -1),
        total_of(arrived[1], sent[1], "fsdp", "rows").astype(BF16).reshape(ctx, pad, -1),
        total_of(arrived[2], sent[2], "fsdp", "rows"),
        total_of(arrived[3], sent[3], "ctx", "rows").astype(BF16),
    ]
    arrived = swap(
        6, *[(x, axis, "rows") for x, axis in zip(sent, ("ctx", "ctx", "ctx", "fsdp"))]
    )
    result_qkv, result_out, gains = [
        total_of(arrived[i], sent[i], "ctx", "rows") for i in range(3)
    ]
    gains = gains[:2, :slim]
    own_gu = lax.dynamic_index_in_dim(sent[3], lax.axis_index("fsdp"), 0, keepdims=False)
    gu_rows = with_own(arrived[3], own_gu, "fsdp")
    gu_rows = gu_rows[:, :slim]
    if dp == 2:
        result_gu = gu_rows.transpose(1, 0, 2).reshape(slim, FF)
    else:
        gu_rows = gu_rows.reshape(fsdp, slim, 2, part).transpose(1, 2, 0, 3).reshape(slim, 2 * FF)
        result_gu = lax.psum_scatter(gu_rows, "dp", scatter_dimension=1, tiled=True)
    return (
        outputs[None],
        grad_inputs[None],
        gains[0],
        gains[1],
        result_qkv[:slim, : w_qkv.shape[1] // dp],
        result_out[:slim, : D // dp],
        result_gu.astype(F32),
        result_down,
    )


def total_of(received, sent, axis, kind):
    me, size = lax.axis_index(axis), lax.axis_size(axis)
    if kind == "all":
        own = sent
    elif kind == "rows":
        own = lax.dynamic_index_in_dim(sent, me, 0, keepdims=False)
    else:
        width = received.shape[-1]
        own = lax.dynamic_slice_in_dim(sent, me * width, width, 1)
    total = own.astype(F32)
    for j in range(size):
        total = total + jnp.where(me == j, 0.0, received[j].astype(F32))
    return total


def with_own(received, own, axis):
    return lax.dynamic_update_index_in_dim(received, own, lax.axis_index(axis), 0)


def in_halves(array, axis, count):
    size = array.shape[axis] // count
    to = -(-size // 128) * 128
    shape = array.shape[:axis] + (count, size) + array.shape[axis + 1 :]
    flat = array.shape[:axis] + (count * to,) + array.shape[axis + 1 :]
    return padded(array.reshape(shape), axis + 1, to).reshape(flat)


def solution(mesh):
    placed = (
        P(("dp", "fsdp"), "ctx", None),
        P(("dp", "fsdp"), "ctx"),
        P(),
        P(),
        P("fsdp", None),
        P("fsdp", None),
        P("fsdp", None),
        P("fsdp", None),
        P(("dp", "fsdp"), "ctx", None),
    )
    return jax.shard_map(
        shards,
        mesh=mesh,
        in_specs=placed,
        out_specs=(
            P(("dp", "fsdp"), "ctx", None),
            P(("dp", "fsdp"), "ctx", None),
            P(("fsdp", "ctx")),
            P(("fsdp", "ctx")),
            P(("fsdp", "ctx"), "dp"),
            P(("fsdp", "ctx"), "dp"),
            P(("fsdp", "ctx"), "dp"),
            P(("fsdp", "ctx"), "dp"),
        ),
        check_vma=False,
    )
```

```python
import functools

import jax
import jax.numpy as jnp
from jax import lax
from jax.experimental import pallas as pl
from jax.experimental.pallas import tpu as pltpu
from jax.sharding import PartitionSpec as P

D = 960
HEADS = 15
KV_HEADS = 5
HD = 64
FF = 2560
GROUP = HEADS // KV_HEADS
KVW = KV_HEADS * HD
EPSILON = 1e-05
F32 = jnp.float32
BF16 = jnp.bfloat16


def dot(a, b, ca, cb):
    return lax.dot_general(a, b, (((ca,), (cb,)), ((), ())), preferred_element_type=F32)


def normalize(values, gain):
    return values * lax.rsqrt(jnp.mean(values * values, axis=-1, keepdims=True) + EPSILON) * gain


def angles_of(places):
    half = HD // 2
    frequency = 10000.0 ** (-jnp.arange(half, dtype=F32) / half)
    angles = frequency[:, None] * places.astype(F32)[None, :]
    return jnp.cos(angles), jnp.sin(angles)


def rotate(values, cosine, sine):
    length = values.shape[1]
    parts = values.reshape(-1, 2, HD // 2, length)
    front, back = parts[:, 0], parts[:, 1]
    turned = jnp.stack([front * cosine - back * sine, back * cosine + front * sine], axis=1)
    return turned.reshape(-1, length)


def keys_first(kv, which):
    pieces = [kv[c, which] for c in range(kv.shape[0])]
    return (
        jnp.concatenate([piece.T for piece in pieces], axis=0),
        jnp.concatenate(pieces, axis=1),
    )


def allowed_of(keys, rows):
    start = lax.axis_index("ctx") * rows
    key_at = lax.broadcasted_iota(jnp.int32, (keys, rows), 0)
    row_at = lax.broadcasted_iota(jnp.int32, (keys, rows), 1)
    return key_at <= row_at + start


MESH = pl.DeviceIdType.MESH


def peer_of(axis, k):
    size = lax.axis_size(axis)
    return lax.rem(lax.axis_index(axis) + k, size)


def greet(axes):
    barrier = pltpu.get_barrier_semaphore()
    count = 0
    for axis in axes:
        for k in range(1, lax.axis_size(axis)):
            pl.semaphore_signal(
                barrier, inc=1, device_id={axis: peer_of(axis, k)}, device_id_type=MESH
            )
            count += 1
    pl.semaphore_wait(barrier, count)


def send(src, dst, sems, at, axis, k):
    copy = pltpu.make_async_remote_copy(
        src_ref=src,
        dst_ref=dst,
        send_sem=sems[0].at[at],
        recv_sem=sems[1].at[at],
        device_id={axis: peer_of(axis, k)},
        device_id_type=MESH,
    )
    copy.start()
    return copy


def swap_kernel(plan, *refs):
    count = len(plan)
    ins, outs = refs[:count], refs[count : 2 * count]
    send_sem, recv_sem = refs[2 * count :]
    greet(sorted({axis for axis, _ in plan}))
    copies, at = [], 0
    for i, (axis, kind) in enumerate(plan):
        me = lax.axis_index(axis)
        for k in range(1, lax.axis_size(axis)):
            there = peer_of(axis, k)
            if kind == "all":
                src = ins[i]
            elif kind == "rows":
                src = ins[i].at[there]
            else:
                width = outs[i].shape[-1]
                src = ins[i].at[:, pl.ds(pl.multiple_of(there * width, 128), width)]
            copies.append(send(src, outs[i].at[me], (send_sem, recv_sem), at, axis, k))
            at += 1
    for copy in copies:
        copy.wait()


def swap(collective_id, *items):
    plan = [(axis, kind) for _, axis, kind in items]

    def shape_of(x, axis, kind):
        size = lax.axis_size(axis)
        if kind == "all":
            return (size,) + x.shape
        if kind == "rows":
            return x.shape
        return (size, x.shape[0], x.shape[1] // size)

    shapes = [jax.ShapeDtypeStruct(shape_of(*item), item[0].dtype) for item in items]
    total = sum(lax.axis_size(axis) - 1 for axis, _ in plan)
    size = sum(shape.size * shape.dtype.itemsize for shape in shapes)
    return pl.pallas_call(
        functools.partial(swap_kernel, plan),
        in_specs=[pl.BlockSpec(memory_space=pl.ANY)] * len(plan),
        out_specs=[pl.BlockSpec(memory_space=pl.ANY)] * len(plan),
        out_shape=shapes,
        scratch_shapes=[
            pltpu.SemaphoreType.DMA((total,)),
            pltpu.SemaphoreType.DMA((total,)),
        ],
        compiler_params=pltpu.CompilerParams(collective_id=collective_id, has_side_effects=True),
        cost_estimate=pl.CostEstimate(flops=0, bytes_accessed=20 * size, transcendentals=0),
    )(*[x for x, _, _ in items])


def front_kernel(
    shared, qkv_in, out_in, gu_in, cot_in, normed, cosine, sine,
    qkv, out_all, gu_all, cot_all, q_ref, kv, att_ref, lse_ref,
    project, local_sem, send_sem, recv_sem, pass_send, pass_recv,
):
    fsdp, ctx = lax.axis_size("fsdp"), lax.axis_size("ctx")
    me, here = lax.axis_index("fsdp"), lax.axis_index("ctx")
    side = lax.axis_index("dp")
    rows = normed.shape[1]
    part = FF // fsdp

    def columns_of(place, device):
        return pl.ds(pl.multiple_of(place * FF + device * part, 128), part)

    def gu_block(place, k):
        columns = columns_of(place, peer_of("fsdp", k))
        mine = pl.ds(place * part, part)
        if shared:
            return gu_in.at[side, :, columns], gu_all.at[me, side, :, mine]
        return gu_in.at[:, :, columns], gu_all.at[me, :, :, mine]

    sems, pass_sems = (send_sem, recv_sem), (pass_send, pass_recv)
    greet(("fsdp", "ctx") + (("dp",) if shared else ()))
    locals_ = [
        pltpu.make_async_copy(qkv_in, qkv.at[me], local_sem.at[0]),
        pltpu.make_async_copy(out_in, out_all.at[me], local_sem.at[1]),
        pltpu.make_async_copy(cot_in, cot_all.at[me], local_sem.at[2]),
    ] + [
        pltpu.make_async_copy(
            gu_in.at[:, :, columns_of(place, me)],
            gu_all.at[me, :, :, place * part : (place + 1) * part],
            local_sem.at[3 + place],
        )
        for place in range(2)
    ]
    for copy in locals_:
        copy.start()
    halves_of = lambda ref: ref.at[side] if shared else ref
    peers = range(1, fsdp)
    first = [
        send(halves_of(qkv_in), halves_of(qkv.at[me]), sems, k - 1, "fsdp", k) for k in peers
    ]
    rest, passed = [], []

    def hand_over(ref, base, arrivals):
        for k, copy in zip(peers, arrivals):
            copy.wait_recv()
            if shared:
                block = ref.at[lax.rem(me - k + fsdp, fsdp), side]
                passed.append(send(block, block, pass_sems, base + k - 1, "dp", 1))

    hand_over(qkv, 0, first)
    base = fsdp - 1
    seconds = [
        send(halves_of(out_in), halves_of(out_all.at[me]), sems, base + k - 1, "fsdp", k)
        for k in peers
    ]
    thirds = [
        send(*gu_block(0, k), sems, 2 * base + k - 1, "fsdp", k) for k in peers
    ]
    fourths = [
        send(*gu_block(1, k), sems, 3 * base + k - 1, "fsdp", k) for k in peers
    ]
    lasts = [send(cot_in, cot_all.at[me], sems, 4 * base + k - 1, "fsdp", k) for k in peers]
    for copy in passed:
        copy.wait_recv()
    locals_[0].wait()
    blocks = 2 * fsdp
    total = jnp.zeros(project.shape[::-1], F32)
    for b in range(blocks):
        total = total + dot(normed[b], qkv[b // 2, b % 2], 1, 0)
    project[...] = total.T
    half = HD // 2
    cos, sin = cosine[...], sine[...]
    mine = kv.at[here]

    def turn(h, carry):
        start = pl.multiple_of(h * HD, HD)
        a = project[pl.ds(start, half), :]
        b = project[pl.ds(start + half, half), :]
        q_ref[pl.ds(start, HD), :] = (
            jnp.concatenate([a * cos - b * sin, b * cos + a * sin], axis=0) * (HD**-0.5)
        ).astype(BF16)
        return carry

    for h in range(KV_HEADS):
        at = D + h * HD
        a, b = project[at : at + half, :], project[at + half : at + HD, :]
        mine[0, h * HD : (h + 1) * HD, :] = jnp.concatenate(
            [a * cos - b * sin, b * cos + a * sin], axis=0
        ).astype(BF16)
    mine[1, :, :] = project[D + KVW :, :].astype(BF16)
    kvs = [
        send(mine, mine, sems, 5 * base + k - 1, "ctx", k) for k in range(1, ctx)
    ]
    lax.fori_loop(0, HEADS, turn, 0)
    hand_over(out_all, base, seconds)
    for copy in kvs:
        copy.wait()
    allowed = allowed_of(ctx * rows, rows)

    def attend(g, carry):
        at = pl.ds(pl.multiple_of(g * HD, HD), HD)
        keys = jnp.concatenate([kv[c, 0, at, :].T for c in range(ctx)], axis=0)
        values_t = jnp.concatenate([kv[c, 1, at, :] for c in range(ctx)], axis=1)
        for h in range(GROUP):
            spot = pl.ds(pl.multiple_of((g * GROUP + h) * HD, HD), HD)
            scores = jnp.where(allowed, dot(keys, q_ref[spot, :], 1, 0), -1e30)
            row_max = jnp.max(scores, axis=0, keepdims=True)
            exponent = jnp.exp(scores - row_max)
            sums = jnp.sum(exponent, axis=0, keepdims=True)
            att = dot(values_t, exponent.astype(BF16), 1, 0) / sums
            att_ref[spot, :] = att.astype(BF16)
            lse_ref[g, h : h + 1, :] = row_max + jnp.log(sums)
        return carry

    lax.fori_loop(0, KV_HEADS, attend, 0)
    for copy in fourths:
        copy.wait_recv()
    hand_over(gu_all, 2 * base, thirds)
    for copy in lasts:
        copy.wait_recv()
    for copy in first + seconds + thirds + fourths + lasts:
        copy.wait_send()
    for i, copy in enumerate(passed):
        copy.wait_send()
        if i >= base:
            copy.wait_recv()
    for copy in locals_[1:]:
        copy.wait()


def front(qkv_in, out_in, gu_in, cot_in, normed, cosine, sine):
    fsdp, ctx, dp = lax.axis_size("fsdp"), lax.axis_size("ctx"), lax.axis_size("dp")
    rows = normed.shape[1]
    columns = qkv_in.shape[-1]
    sends = 5 * (fsdp - 1) + ctx - 1
    anywhere, vmem = pl.BlockSpec(memory_space=pl.ANY), pl.BlockSpec(memory_space=pltpu.VMEM)
    shape = jax.ShapeDtypeStruct
    return pl.pallas_call(
        functools.partial(front_kernel, dp == 2),
        in_specs=[anywhere] * 4 + [vmem] * 3,
        out_specs=[vmem] * 8,
        out_shape=[
            shape((fsdp,) + qkv_in.shape, BF16),
            shape((fsdp,) + out_in.shape, BF16),
            shape((fsdp,) + gu_in.shape[:2] + (2 * FF // fsdp,), BF16),
            shape((fsdp,) + cot_in.shape, BF16),
            shape((D, rows), BF16),
            shape((ctx, 2, KVW, rows), BF16),
            shape((D, rows), BF16),
            shape((KV_HEADS, GROUP, rows), F32),
        ],
        scratch_shapes=[
            pltpu.VMEM((columns, rows), F32),
            pltpu.SemaphoreType.DMA((5,)),
            pltpu.SemaphoreType.DMA((sends,)),
            pltpu.SemaphoreType.DMA((sends,)),
            pltpu.SemaphoreType.DMA((3 * (fsdp - 1),)),
            pltpu.SemaphoreType.DMA((3 * (fsdp - 1),)),
        ],
        compiler_params=pltpu.CompilerParams(
            collective_id=0, has_side_effects=True, vmem_limit_bytes=48 * 2**20
        ),
        cost_estimate=pl.CostEstimate(
            flops=10**9, bytes_accessed=10**8, transcendentals=10**6
        ),
    )(qkv_in, out_in, gu_in, cot_in, normed, cosine, sine)


def back_kernel(
    q_ref, kv, g_ref, lse_ref, down_in, dq_ref, dkv, kv_out, down_out,
    down_send, down_recv, kv_send, kv_recv,
):
    fsdp, ctx = lax.axis_size("fsdp"), lax.axis_size("ctx")
    me, here = lax.axis_index("fsdp"), lax.axis_index("ctx")
    rows = q_ref.shape[1]
    greet(("fsdp", "ctx"))
    downs = [
        send(
            down_in.at[peer_of("fsdp", k)], down_out.at[me], (down_send, down_recv), k - 1, "fsdp", k
        )
        for k in range(1, fsdp)
    ]
    allowed = allowed_of(ctx * rows, rows)

    def kv_copy(g, k):
        at = pl.ds(pl.multiple_of(g * HD, HD), HD)
        spot = g * (ctx - 1) + k - 1
        there = peer_of("ctx", k)
        return pltpu.make_async_remote_copy(
            src_ref=dkv.at[there, :, at, :],
            dst_ref=kv_out.at[here, :, at, :],
            send_sem=kv_send.at[spot],
            recv_sem=kv_recv.at[spot],
            device_id={"ctx": there},
            device_id_type=MESH,
        )

    def attend_back(g, carry):
        at = pl.ds(pl.multiple_of(g * HD, HD), HD)
        keys = jnp.concatenate([kv[c, 0, at, :].T for c in range(ctx)], axis=0)
        keys_t = jnp.concatenate([kv[c, 0, at, :] for c in range(ctx)], axis=1)
        values = jnp.concatenate([kv[c, 1, at, :].T for c in range(ctx)], axis=0)
        dk = jnp.zeros((HD, ctx * rows), F32)
        dv = jnp.zeros((HD, ctx * rows), F32)
        for h in range(GROUP):
            spot = pl.ds(pl.multiple_of((g * GROUP + h) * HD, HD), HD)
            q, grad = q_ref[spot, :], g_ref[spot, :]
            scores = jnp.where(allowed, dot(keys, q, 1, 0), -1e30)
            prob = jnp.exp(scores - lse_ref[g, h : h + 1, :])
            dprob = dot(values, grad, 1, 0)
            inner = jnp.sum(dprob * prob, axis=0, keepdims=True)
            ds = (prob * (dprob - inner)).astype(BF16)
            dq_ref[spot, :] = dot(keys_t, ds, 1, 0) * (HD**-0.5)
            dk = dk + dot(q, ds, 1, 1)
            dv = dv + dot(grad, prob.astype(BF16), 1, 1)
        for c in range(ctx):
            dkv[c, 0, at, :] = dk[:, c * rows : (c + 1) * rows].astype(BF16)
            dkv[c, 1, at, :] = dv[:, c * rows : (c + 1) * rows].astype(BF16)
        for k in range(1, ctx):
            kv_copy(g, k).start()
        return carry

    def finish(g, carry):
        for k in range(1, ctx):
            kv_copy(g, k).wait()
        return carry

    lax.fori_loop(0, KV_HEADS, attend_back, 0)
    lax.fori_loop(0, KV_HEADS, finish, 0)
    for copy in downs:
        copy.wait()


def back(q, kv, g, lse, down_part):
    parts, rows = kv.shape[0], q.shape[1]
    fsdp = down_part.shape[0]
    work = parts * rows * rows * HD * HEADS
    anywhere, vmem = pl.BlockSpec(memory_space=pl.ANY), pl.BlockSpec(memory_space=pltpu.VMEM)
    shape = jax.ShapeDtypeStruct
    return pl.pallas_call(
        back_kernel,
        in_specs=[vmem] * 4 + [anywhere],
        out_specs=[vmem] * 3 + [anywhere],
        out_shape=[
            shape((D, rows), F32),
            shape(kv.shape, BF16),
            shape(kv.shape, BF16),
            shape(down_part.shape, BF16),
        ],
        scratch_shapes=[
            pltpu.SemaphoreType.DMA((fsdp - 1,)),
            pltpu.SemaphoreType.DMA((fsdp - 1,)),
            pltpu.SemaphoreType.DMA((KV_HEADS * (parts - 1),)),
            pltpu.SemaphoreType.DMA((KV_HEADS * (parts - 1),)),
        ],
        compiler_params=pltpu.CompilerParams(
            collective_id=3, has_side_effects=True, vmem_limit_bytes=48 * 2**20
        ),
        cost_estimate=pl.CostEstimate(
            flops=40 * work, bytes_accessed=5 * 2**20, transcendentals=work // HD
        ),
    )(q, kv, g, lse, down_part)


def padded(array, axis, to):
    widths = [(0, 0)] * array.ndim
    widths[axis] = (0, to - array.shape[axis])
    return jnp.pad(array, widths)


def shards(tokens, positions, gain_attn, gain_mlp, w_qkv, w_out, w_gu, w_down, cotangent):
    rows = tokens.shape[1]
    fsdp, ctx, dp = lax.axis_size("fsdp"), lax.axis_size("ctx"), lax.axis_size("dp")
    part = FF // fsdp
    own = D // fsdp
    slim = D // (fsdp * ctx)
    half, wide_half = own // 2, -(-own // 2 // 128) * 128
    pad = -(-slim // 16) * 16
    wide = w_qkv.shape[1] // dp
    inputs = tokens[0].astype(F32)
    cosine, sine = angles_of(positions[0])
    normed = normalize(inputs, gain_attn).astype(BF16)
    normed_cut = padded(normed.reshape(rows, 2 * fsdp, half).transpose(1, 0, 2), 2, wide_half)
    qkv_all, out_all, gu_all, cot_all, queries, every_kv, attended, lse = front(
        padded(w_qkv.reshape(2, half, -1), 1, wide_half),
        padded(w_out.reshape(2, half, D), 1, wide_half),
        padded(w_gu.reshape(2, half, 2 * FF), 1, wide_half),
        cotangent[0],
        normed_cut,
        cosine,
        sine,
    )
    full_qkv = qkv_all[:, :, :half].reshape(D, -1)
    full_out = out_all[:, :, :half].reshape(D, D)
    gu_part = gu_all[:, :, :half].reshape(D, 2 * part)
    cot_all = cot_all.reshape(fsdp * rows, D)

    hidden = inputs + dot(attended, full_out, 0, 0)
    normed_two = normalize(hidden, gain_mlp).astype(BF16)
    (two_all,) = swap(1, (normed_two, "fsdp", "all"))
    two_all = with_own(two_all, normed_two, "fsdp").reshape(fsdp * rows, D)
    gate_up = dot(two_all, gu_part, 1, 0)
    gate, up = gate_up[:, :part], gate_up[:, part:]
    activated, swish_back = jax.vjp(lambda a, b: jax.nn.silu(a) * b, gate, up)
    activated = activated.astype(BF16)
    grad_activated = dot(cot_all, w_down, 1, 1)
    grad_gate, grad_up = swish_back(grad_activated)
    grad_gate_up = jnp.concatenate([grad_gate, grad_up], axis=1).astype(BF16)
    two_part = dot(grad_gate_up, gu_part, 1, 1).astype(BF16).reshape(fsdp, rows, D)
    down_part = dot(activated, w_down, 1, 0).astype(BF16).reshape(fsdp, rows, D)
    grad_down = dot(activated, in_halves(cot_all, 1, dp), 0, 0).astype(BF16)

    def spread(array):
        array = array.reshape(-1, fsdp * ctx, slim)
        return padded(array, 2, pad).reshape(-1, fsdp * ctx * pad)

    grad_gu = dot(spread(two_all), grad_gate_up, 0, 0).astype(BF16)
    grad_down = grad_down.reshape(ctx, part // ctx, -1)
    if dp == 2:
        two_sum, down_grads, gu_sum = swap(
            2, (two_part, "fsdp", "rows"), (grad_down, "ctx", "rows"), (grad_gu, "dp", "columns")
        )
        gu_cols = total_of(gu_sum, grad_gu, "dp", "columns").astype(BF16)
    else:
        two_sum, down_grads = swap(2, (two_part, "fsdp", "rows"), (grad_down, "ctx", "rows"))
        gu_cols = grad_gu
    grad_two = total_of(two_sum, two_part, "fsdp", "rows")
    down_grads = total_of(down_grads, grad_down, "ctx", "rows").astype(BF16)
    gu_cols = gu_cols.reshape(fsdp, ctx, pad, -1).transpose(1, 0, 2, 3)

    grad_rows = cotangent[0].astype(F32)
    _, norm_back_two = jax.vjp(normalize, hidden, gain_mlp)
    grad_hidden_part, grad_gain_mlp = norm_back_two(grad_two)
    grad_hidden = grad_rows + grad_hidden_part
    grad_attn = grad_hidden.astype(BF16)
    grad_attended = dot(full_out, grad_attn, 1, 1).astype(BF16)
    attended_wide = padded(attended.reshape(fsdp * ctx, slim, rows), 1, pad).reshape(-1, rows)
    grad_out = dot(attended_wide, in_halves(grad_attn, 1, dp), 1, 0).astype(BF16)
    grad_queries, kv_grads, kv_sum, down_sum = back(
        queries, every_kv, grad_attended, lse, down_part
    )
    own_kv = total_of(kv_sum, kv_grads, "ctx", "rows").reshape(2 * KVW, rows)
    outputs = hidden + total_of(down_sum, down_part, "fsdp", "rows")
    grad_project = jnp.concatenate(
        [
            rotate(grad_queries, cosine, -sine),
            rotate(own_kv[:KVW], cosine, -sine),
            own_kv[KVW:],
        ],
        axis=0,
    ).astype(BF16)
    grad_normed = dot(grad_project, full_qkv, 0, 1)
    grad_qkv = dot(spread(normed), in_halves(grad_project, 0, dp), 0, 1).astype(BF16)
    _, norm_back_one = jax.vjp(normalize, inputs, gain_attn)
    grad_input_part, grad_gain_attn = norm_back_one(grad_normed)
    grad_inputs = grad_hidden + grad_input_part

    gains = jnp.stack([grad_gain_attn, grad_gain_mlp]).reshape(2, fsdp, ctx, slim)
    gains = padded(padded(gains.transpose(1, 2, 0, 3), 2, 8), 3, 128)
    arrived = swap(
        4,
        (grad_qkv, "dp", "columns"),
        (grad_out, "dp", "columns"),
        (gains, "dp", "all"),
        (down_grads, "dp", "columns"),
    )
    result_down = total_of(arrived[3], down_grads, "dp", "columns")[:, : D // dp]
    sent = [
        jnp.concatenate(
            [
                total_of(arrived[0], grad_qkv, "dp", "columns")[:, :wide],
                total_of(arrived[1], grad_out, "dp", "columns")[:, : D // dp],
            ],
            axis=1,
        ).astype(BF16).reshape(fsdp, ctx * pad, -1),
        total_of(arrived[2], gains, "dp", "all"),
        gu_cols,
    ]
    arrived = swap(
        5, *[(x, axis, "rows") for x, axis in zip(sent, ("fsdp", "fsdp", "ctx"))]
    )
    sent = [
        total_of(arrived[0], sent[0], "fsdp", "rows").astype(BF16).reshape(ctx, pad, -1),
        total_of(arrived[1], sent[1], "fsdp", "rows"),
        total_of(arrived[2], sent[2], "ctx", "rows").astype(BF16),
    ]
    arrived = swap(
        6, *[(x, axis, "rows") for x, axis in zip(sent, ("ctx", "ctx", "fsdp"))]
    )
    both, gains = [total_of(arrived[i], sent[i], "ctx", "rows") for i in range(2)]
    gains = gains[:2, :slim]
    own_gu = lax.dynamic_index_in_dim(sent[2], lax.axis_index("fsdp"), 0, keepdims=False)
    gu_rows = with_own(arrived[2], own_gu, "fsdp")
    gu_rows = gu_rows[:, :slim]
    if dp == 2:
        result_gu = gu_rows.transpose(1, 0, 2).reshape(slim, FF)
    else:
        gu_rows = gu_rows.reshape(fsdp, slim, 2, part).transpose(1, 2, 0, 3).reshape(slim, 2 * FF)
        result_gu = lax.psum_scatter(gu_rows, "dp", scatter_dimension=1, tiled=True)
    return (
        outputs[None],
        grad_inputs[None],
        gains[0],
        gains[1],
        both[:slim, :wide],
        both[:slim, wide:],
        result_gu.astype(F32),
        result_down,
    )


def total_of(received, sent, axis, kind):
    me, size = lax.axis_index(axis), lax.axis_size(axis)
    if kind == "all":
        own = sent
    elif kind == "rows":
        own = lax.dynamic_index_in_dim(sent, me, 0, keepdims=False)
    else:
        width = received.shape[-1]
        own = lax.dynamic_slice_in_dim(sent, me * width, width, 1)
    total = own.astype(F32)
    for j in range(size):
        total = total + jnp.where(me == j, 0.0, received[j].astype(F32))
    return total


def with_own(received, own, axis):
    return lax.dynamic_update_index_in_dim(received, own, lax.axis_index(axis), 0)


def in_halves(array, axis, count):
    size = array.shape[axis] // count
    to = -(-size // 128) * 128
    shape = array.shape[:axis] + (count, size) + array.shape[axis + 1 :]
    flat = array.shape[:axis] + (count * to,) + array.shape[axis + 1 :]
    return padded(array.reshape(shape), axis + 1, to).reshape(flat)


def solution(mesh):
    placed = (
        P(("dp", "fsdp"), "ctx", None),
        P(("dp", "fsdp"), "ctx"),
        P(),
        P(),
        P("fsdp", None),
        P("fsdp", None),
        P("fsdp", None),
        P("fsdp", None),
        P(("dp", "fsdp"), "ctx", None),
    )
    return jax.shard_map(
        shards,
        mesh=mesh,
        in_specs=placed,
        out_specs=(
            P(("dp", "fsdp"), "ctx", None),
            P(("dp", "fsdp"), "ctx", None),
            P(("fsdp", "ctx")),
            P(("fsdp", "ctx")),
            P(("fsdp", "ctx"), "dp"),
            P(("fsdp", "ctx"), "dp"),
            P(("fsdp", "ctx"), "dp"),
            P(("fsdp", "ctx"), "dp"),
        ),
        check_vma=False,
    )
```
